512 devices in a mesh: expert: 128 (over z, y, core), group: 4 (over x).
Axes of the slice: x: 4, y: 4, z: 16, core: 2. Of those that a mesh axis runs over, the one named last changes fastest.
Arguments:
- tokens: bfloat16 [65536, 1024], P(('expert', 'group')), may hold values from -6 to 6
- out_grad: bfloat16 [65536, 1024], P(('expert', 'group')), may hold values from -6 to 6
- w_router: bfloat16 [1024, 256], P('group', 'expert'), may hold values from -0.1875 to 0.1875
- w_in: bfloat16 [128, 1024, 2048], P('expert', None, 'group'), may hold values from -0.1875 to 0.1875
- w_out: bfloat16 [128, 2048, 1024], P('expert', 'group'), may hold values from -0.09375 to 0.09375
- expert_ids: int32 [65536, 2], P(('expert', 'group')), may hold values from 0 to 255, as said below
- slot_ids: int32 [65536, 2], P(('expert', 'group')), may hold values from 0 to 1, as said below
- keep_mask: int32 [65536, 2], P(('expert', 'group')), may hold values 0 or 1
Outputs:
- in_grad: bfloat16 [65536, 1024], P(('expert', 'group'))
- w_in_grad: bfloat16 [128, 1024, 2048], P('expert', None, 'group')
- w_out_grad: bfloat16 [128, 2048, 1024], P('expert', 'group')
- router_grad: float32 [1024, 256], P('group', 'expert')
The draws below stay inside these ranges and needn't reach their ends.
Inputs may be any that keep to these rules, and one draw needn't show every extreme that they name: `expert_ids`: the two ids of a token differ. Among the tokens of one device no expert is named more than 2 times, and in every draw some expert below 64 is named 2 times by the tokens of every device. slot_ids[t, 0] is 0; slot_ids[t, 1] is 1 exactly when the second expert of token t is also the first expert of another token of the same device, else 0; so on one device no two choices share both expert and slot.
All inputs are finite; a program needn't handle non-finite values. No bound on the sum of `keep_mask` on one device may be relied on, other than what follows from the above.
Results may differ from the reference program's by a relative error of at most 0.015.
Values may be sent and summed in bfloat16 or wider, within the bound.
No kernel may reach another device: no remote copies, remote signals or barrier semaphores. Data moves between devices by JAX's collectives and lax.ppermute only.
A program may use at most 64 MiB of HBM per device.

```python
import jax
import jax.numpy as jnp
from jax import lax

D = 1024
HID = 4096
CANDIDATE_SPECS = 256
TOP = 2
CAP = 2
SPLIT = 2
TOK = 128
RESIDENT_SPECS = 64
HS = 512
TOKENS = 65536
N_GROUP = 4


def route_table(key):
    block_count = TOKENS // TOK
    shared = jax.random.fold_in(key, 7)
    favoured_specialist = jax.random.randint(jax.random.fold_in(shared, 1), (), 0, RESIDENT_SPECS)
    entropy_integers = jax.random.randint(jax.random.fold_in(shared, 2), (CANDIDATE_SPECS,), 0, 8)
    uniform_samples = jnp.arange(CANDIDATE_SPECS, dtype=jnp.int32)
    favour_increment = jnp.where(uniform_samples == favoured_specialist, 2, jnp.where((entropy_integers == 0) & (uniform_samples < RESIDENT_SPECS), 1, 0))
    ordering_perturbation = jax.random.randint(jax.random.fold_in(key, 8), (block_count, CANDIDATE_SPECS), 0, 65536)
    specialist_logit = (favour_increment[None, :] * 65536 + ordering_perturbation) * CANDIDATE_SPECS + uniform_samples[None, :]
    ranking = jnp.argsort(-specialist_logit, axis=1).astype(jnp.int32)
    offsets = jax.random.randint(jax.random.fold_in(key, 9), (block_count, 1), 1, TOK // 2 + 1)
    places = jnp.arange(TOK, dtype=jnp.int32)[None, :]
    first_rank = jnp.broadcast_to(places, (block_count, TOK))
    second_rank = (places - offsets) % CANDIDATE_SPECS
    first_ids = jnp.take_along_axis(ranking, first_rank, axis=1)
    second_ids = jnp.take_along_axis(ranking, second_rank, axis=1)
    second_slot = jnp.broadcast_to((places >= offsets).astype(jnp.int32), (block_count, TOK))
    order_noise = jax.random.randint(jax.random.fold_in(key, 10), (block_count, TOK), 0, 65536) * TOK + places
    shuffle = jnp.argsort(order_noise, axis=1).astype(jnp.int32)
    first_ids = jnp.take_along_axis(first_ids, shuffle, axis=1)
    second_ids = jnp.take_along_axis(second_ids, shuffle, axis=1)
    second_slot = jnp.take_along_axis(second_slot, shuffle, axis=1)
    id_table = jnp.stack([first_ids, second_ids], axis=2).reshape(TOKENS, 2).astype(jnp.int32)
    slot_table = jnp.stack([jnp.zeros_like(second_slot), second_slot], axis=2).reshape(TOKENS, 2).astype(jnp.int32)
    return (id_table, slot_table)


def draw_expert_ids(key, part):
    id_table, slot_table = route_table(key)
    return id_table


def draw_slot_ids(key, part):
    id_table, slot_table = route_table(key)
    return slot_table


def plant(drawn, stream_key, least, high):
    longest = drawn.shape.index(max(drawn.shape))
    spots = []
    for shift in (0, 1):
        where = [jax.random.randint(jax.random.fold_in(stream_key, axis), (), 0, length) for axis, length in enumerate(drawn.shape)]
        where[longest] = (where[longest] + shift) % drawn.shape[longest]
        spots.append(tuple(where))
    return drawn.at[spots[0]].set(least).at[spots[1]].set(high)


def shard_levels(own_key, dims, shards, least, top_value):
    loudness, own = 1.0, jax.random.fold_in(own_key, 6)
    for position, blocks in shards:
        steps = jnp.exp(jax.random.uniform(jax.random.fold_in(own, position), (blocks,), jnp.float32, least / len(shards), top_value / len(shards)))
        loudness = loudness * jnp.repeat(steps, dims[position] // blocks).reshape([-1 if axis == position else 1 for axis in range(len(dims))])
    return loudness


def noise(key, dims, width, limit, pieces=(), kind=jnp.bfloat16):
    gain = shard_levels(key, dims, pieces, -0.22, 0.18) if pieces else 1.0
    drawn = jax.random.normal(key, dims, jnp.float32) * width * gain
    return jnp.minimum(jnp.maximum(drawn, -limit), limit).astype(kind)


def setup_inputs(seed: int = 0) -> dict:
    streams_of = jax.random.split(jax.random.key(seed), 9)
    tokens = noise(streams_of[0], (TOKENS, D), 1.0, 6.0, ((0, 512),))
    out_grad = noise(streams_of[1], (TOKENS, D), 1.0, 6.0, ((0, 512),))
    w_router = noise(streams_of[2], (D, CANDIDATE_SPECS), D ** -0.5, 0.1875, ((0, 4), (1, 128)))
    w_in = noise(streams_of[3], (RESIDENT_SPECS * SPLIT, D, HID // SPLIT), D ** -0.5, 0.1875, ((0, 128), (2, 4)))
    w_out = noise(streams_of[4], (RESIDENT_SPECS * SPLIT, HID // SPLIT, D), HID ** -0.5, 0.09375, ((0, 128), (1, 4)))
    expert_ids = draw_expert_ids(jax.random.fold_in(streams_of[8], 71), 0)
    slot_ids = draw_slot_ids(jax.random.fold_in(streams_of[8], 71), 0)
    keep_mask = plant((jax.random.randint(streams_of[7], (TOKENS, TOP), 0, 5) < 4).astype(jnp.int32), jax.random.fold_in(streams_of[7], 1), 0, 1)
    return dict(tokens=tokens, out_grad=out_grad, w_router=w_router, w_in=w_in, w_out=w_out, expert_ids=expert_ids, slot_ids=slot_ids, keep_mask=keep_mask)


def gelu_parts(pre_act):
    cubic_term = 0.044715 * pre_act * pre_act * pre_act
    tanh_value = jnp.tanh(0.7978845608028654 * (pre_act + cubic_term))
    gelu_value = 0.5 * pre_act * (1.0 + tanh_value)
    gelu_slope = 0.5 * (1.0 + tanh_value) + 0.5 * pre_act * (1.0 - tanh_value * tanh_value) * 0.7978845608028654 * (1.0 + 3.0 * 0.044715 * pre_act * pre_act)
    return gelu_value, gelu_slope


def expert_backward(inputs):
    x_rows, dy_rows, gate_rows, in_blocks, out_blocks = inputs
    x_wide = x_rows.astype(jnp.float32)
    dy_wide = dy_rows.astype(jnp.float32)
    in_wide = in_blocks.astype(jnp.float32)
    out_wide = out_blocks.astype(jnp.float32)
    gate_wide = gate_rows.astype(jnp.float32)
    pre_act = jnp.einsum("rd,bdh->brh", x_wide, in_wide, precision=lax.Precision.HIGHEST)
    gelu_value, gelu_slope = gelu_parts(pre_act)
    back_up = jnp.einsum("rd,bhd->brh", dy_wide, out_wide, precision=lax.Precision.HIGHEST)
    gate_grad = jnp.sum(jnp.sum(back_up * gelu_value, axis=2), axis=0)
    pre_grad = lax.optimization_barrier((gate_wide[None, :, None] * back_up * gelu_slope).astype(jnp.bfloat16))
    scaled_grad = lax.optimization_barrier((gate_wide[:, None] * dy_wide).astype(jnp.bfloat16))
    hidden_round = lax.optimization_barrier(gelu_value.astype(jnp.bfloat16))
    grad_in = jnp.einsum("rd,brh->bdh", x_wide, pre_grad.astype(jnp.float32), precision=lax.Precision.HIGHEST).astype(jnp.bfloat16)
    grad_out = jnp.einsum("brh,rd->bhd", hidden_round.astype(jnp.float32), scaled_grad.astype(jnp.float32), precision=lax.Precision.HIGHEST).astype(jnp.bfloat16)
    row_parts = lax.optimization_barrier(jnp.einsum("brh,bdh->brd", pre_grad.astype(jnp.float32), in_wide, precision=lax.Precision.HIGHEST).astype(jnp.bfloat16))
    row_grad = jnp.sum(row_parts.astype(jnp.float32), axis=0)
    return row_grad, gate_grad, grad_in, grad_out


def reference(tokens, out_grad, w_router, w_in, w_out, expert_ids, slot_ids, keep_mask):
    total_rows = tokens.shape[0]
    block_count = total_rows // TOK
    row_count = block_count * CAP
    logits = jnp.dot(tokens, w_router, preferred_element_type=jnp.float32)
    chosen = jnp.take_along_axis(logits, expert_ids, axis=1)
    logit_gap = chosen[:, 0] - chosen[:, 1]
    combine = jnp.stack([jax.nn.sigmoid(logit_gap), jax.nn.sigmoid(-logit_gap)], axis=1)
    active = (keep_mask == 1) & (expert_ids < RESIDENT_SPECS)
    rows_index = ((jnp.arange(total_rows, dtype=jnp.int32) // TOK)[:, None] * CAP + slot_ids).astype(jnp.int32)
    target = jnp.where(active, expert_ids, RESIDENT_SPECS).astype(jnp.int32)
    x_buf = jnp.zeros((RESIDENT_SPECS, row_count, D), jnp.bfloat16).at[target, rows_index].set(jnp.broadcast_to(tokens[:, None, :], (total_rows, TOP, D)), mode="drop")
    dy_buf = jnp.zeros((RESIDENT_SPECS, row_count, D), jnp.bfloat16).at[target, rows_index].set(jnp.broadcast_to(out_grad[:, None, :], (total_rows, TOP, D)), mode="drop")
    gate_buf = jnp.zeros((RESIDENT_SPECS, row_count), jnp.bfloat16).at[target, rows_index].set(combine.astype(jnp.bfloat16), mode="drop")
    in_blocks = w_in.reshape(RESIDENT_SPECS, SPLIT, D, N_GROUP, HS).transpose(0, 1, 3, 2, 4).reshape(RESIDENT_SPECS, SPLIT * N_GROUP, D, HS)
    out_blocks = w_out.reshape(RESIDENT_SPECS, SPLIT * N_GROUP, HS, D)
    row_grad, gate_grad, grad_in, grad_out = lax.map(expert_backward, (x_buf, dy_buf, gate_buf, in_blocks, out_blocks))
    w_in_grad = grad_in.reshape(RESIDENT_SPECS, SPLIT, N_GROUP, D, HS).transpose(0, 1, 3, 2, 4).reshape(RESIDENT_SPECS * SPLIT, D, HID // SPLIT)
    w_out_grad = grad_out.reshape(RESIDENT_SPECS * SPLIT, HID // SPLIT, D)
    safe_target = jnp.minimum(target, RESIDENT_SPECS - 1).astype(jnp.int32)
    picked_rows = row_grad[safe_target, rows_index]
    expert_part = jnp.sum(jnp.where(active[:, :, None], picked_rows, jnp.float32(0.0)), axis=1)
    gate_back = jnp.where(active, gate_grad[safe_target, rows_index], jnp.float32(0.0))
    gate_slope = combine[:, 0] * combine[:, 1] * (gate_back[:, 0] - gate_back[:, 1])
    uniform_samples = jnp.arange(CANDIDATE_SPECS, dtype=jnp.int32)
    first_hot = (expert_ids[:, 0:1] == uniform_samples[None, :]).astype(jnp.float32)
    second_hot = (expert_ids[:, 1:2] == uniform_samples[None, :]).astype(jnp.float32)
    logit_grad = first_hot * gate_slope[:, None] - second_hot * gate_slope[:, None]
    router_part = jnp.dot(logit_grad, w_router.astype(jnp.float32).T, precision=lax.Precision.HIGHEST)
    in_grad = (expert_part + router_part).astype(jnp.bfloat16)
    router_grad = jnp.dot(tokens.astype(jnp.float32).T, logit_grad, precision=lax.Precision.HIGHEST)
    return (in_grad, w_in_grad, w_out_grad, router_grad)
```

```python
import jax
import jax.numpy as jnp
from jax import lax
from jax.sharding import Mesh
from jax.sharding import PartitionSpec as P

CAP = 2
SPLIT = 2
SWAP = [(0, 1), (1, 0)]
BF = jnp.bfloat16
F32 = jnp.float32


def gelu_parts(pre_act):
    cubic_term = 0.044715 * pre_act * pre_act * pre_act
    tanh_value = jnp.tanh(0.7978845608028654 * (pre_act + cubic_term))
    gelu_value = 0.5 * pre_act * (1.0 + tanh_value)
    gelu_slope = 0.5 * (1.0 + tanh_value) + 0.5 * pre_act * (
        1.0 - tanh_value * tanh_value
    ) * 0.7978845608028654 * (1.0 + 3.0 * 0.044715 * pre_act * pre_act)
    return (gelu_value, gelu_slope)


def dot(a, b, dims):
    return lax.dot_general(a, b, (dims, ((), ())), preferred_element_type=F32)


def shift_group(value, step):
    count = lax.axis_size("group")
    return lax.ppermute(value, "group", [(i, (i + step) % count) for i in range(count)])


def swap_cores(value):
    return lax.ppermute(value, "core", SWAP)


def body(tokens, out_grad, w_router, w_in, w_out, expert_ids, slot_ids, keep_mask):
    chips = lax.axis_size("chip")
    groups = lax.axis_size("group")
    chip = lax.axis_index("chip")
    core = lax.axis_index("core")
    group = lax.axis_index("group")
    width = tokens.shape[1]
    slot_count = chips * CAP
    part = w_router.shape[0]
    w_in_own, w_out_own = w_in[0], w_out[0]
    w_in_sib, w_out_sib = swap_cores(w_in_own), swap_cores(w_out_own)

    active = (keep_mask == 1) & (expert_ids < chips)
    slot_code = jnp.where(active, expert_ids * CAP + slot_ids, -1)
    slot_axis = jnp.arange(slot_count, dtype=jnp.int32)
    first = slot_axis[:, None] == slot_code[None, :, 0]
    second = slot_axis[:, None] == slot_code[None, :, 1]
    place = (first | second).astype(BF)
    other = jnp.sum(
        jnp.where(first, expert_ids[None, :, 1], 0) + jnp.where(second, expert_ids[None, :, 0], 0),
        axis=1,
    )
    token_slots = dot(place, tokens, ((1,), (0,))).astype(BF)
    grad_slots = dot(place, out_grad, ((1,), (0,))).astype(BF)
    meta = jnp.broadcast_to(other.astype(BF)[:, None], (slot_count, 128))
    router_rows = jnp.broadcast_to(w_router.T[None], (chips, CAP, part)).reshape(slot_count, part)
    send = jnp.concatenate([token_slots, grad_slots, router_rows, meta], axis=1)
    wide = send.shape[1]
    recv = lax.all_to_all(
        send.reshape(chips, CAP, wide), "chip", split_axis=0, concat_axis=0, tiled=True
    ).reshape(slot_count, wide)

    blocks = [recv, shift_group(recv, -1), shift_group(recv, 2), shift_group(recv, 1)]
    rows = jnp.concatenate(blocks, axis=0)
    x_rows, dy_rows = rows[:, :width], rows[:, width : 2 * width]
    other_id = rows[:, 2 * width + part : 2 * width + part + 1].astype(jnp.int32)

    turned = jnp.concatenate([b[:, 2 * width : 2 * width + part] for b in blocks] * 2, axis=1)
    router_own = lax.dynamic_slice_in_dim(turned, (groups - group) % groups * part, width, axis=1)
    router = jnp.concatenate([router_own, swap_cores(router_own)], axis=0)
    columns = router.shape[0]

    def column_of(expert):
        mine = (expert // CAP) % SPLIT == core
        return jnp.where(mine, 0, columns // 2) + expert // (CAP * SPLIT) * CAP + expert % CAP

    column_axis = jnp.arange(columns, dtype=jnp.int32)[None, :]
    sign = (column_axis == column_of(chip)).astype(F32) - (
        column_axis == column_of(other_id)
    ).astype(F32)
    logits = dot(x_rows, router, ((1,), (1,)))
    gap = jnp.sum(logits * sign, axis=1, keepdims=True)
    combine = jax.nn.sigmoid(gap)
    cross = combine * jax.nn.sigmoid(-gap)
    gate = combine.astype(BF).astype(F32)
    scaled = (gate * dy_rows.astype(F32)).astype(BF)

    gate_grad = 0.0
    row_part = 0.0
    halves = []
    for w_a, w_b in ((w_in_own, w_out_own), (w_in_sib, w_out_sib)):
        gelu_value, gelu_slope = gelu_parts(dot(x_rows, w_a, ((1,), (0,))))
        back_up = dot(dy_rows, w_b, ((1,), (1,)))
        gate_grad = gate_grad + jnp.sum(back_up * gelu_value, axis=1, keepdims=True)
        pre_grad = (gate * back_up * gelu_slope).astype(BF)
        row_part = row_part + dot(pre_grad, w_a, ((1,), (1,)))
        halves.append((pre_grad, gelu_value.astype(BF)))
    logit_grad = (cross * gate_grad * sign).astype(BF)
    row_part = row_part + dot(logit_grad, router, ((1,), (0,)))

    router_part = dot(logit_grad, x_rows, ((0,), (0,)))
    half = columns // 2
    router_part = router_part[:half] + swap_cores(router_part[half:].astype(BF)).astype(F32)
    router_part = router_part.astype(BF)
    router_turned = lax.dynamic_slice_in_dim(
        jnp.concatenate([router_part, router_part], axis=1), group * part, width, axis=1
    )
    row_part = row_part.astype(BF)
    back = [
        jnp.concatenate(
            [
                row_part[i * slot_count : (i + 1) * slot_count],
                router_turned[:, i * part : (i + 1) * part],
            ],
            axis=1,
        )
        for i in range(groups)
    ]
    total = (
        back[0].astype(F32)
        + shift_group(back[1], 1).astype(F32)
        + shift_group(back[2], 2).astype(F32)
        + shift_group(back[3], -1).astype(F32)
    ).astype(BF)
    home = lax.all_to_all(
        total.reshape(chips, CAP, width + part), "chip", split_axis=0, concat_axis=0, tiled=True
    )
    rows_home = home[:, :, :width].reshape(slot_count, width)
    in_grad = dot(place, rows_home, ((0,), (0,))).astype(BF)
    router_grad = jnp.sum(home[:, :, width:].astype(F32), axis=0).T

    (pre_own, hid_own), (pre_sib, hid_sib) = halves
    in_sib = swap_cores(dot(x_rows, pre_sib, ((0,), (0,))).astype(BF))
    out_sib = swap_cores(dot(hid_sib, scaled, ((0,), (0,))).astype(BF))
    w_in_grad = (dot(x_rows, pre_own, ((0,), (0,))) + in_sib.astype(F32)).astype(BF)[None]
    w_out_grad = (dot(hid_own, scaled, ((0,), (0,))) + out_sib.astype(F32)).astype(BF)[None]
    return (in_grad, w_in_grad, w_out_grad, router_grad)


def solution(mesh):
    experts, groups = mesh.devices.shape
    cut = Mesh(
        mesh.devices.reshape(experts // SPLIT, SPLIT, groups), ("chip", "core", "group")
    )
    by_token = P(("chip", "core", "group"), None)
    by_router = P("group", ("chip", "core"))
    by_in = P(("chip", "core"), None, "group")
    by_out = P(("chip", "core"), "group", None)
    return jax.shard_map(
        body,
        mesh=cut,
        in_specs=(by_token, by_token, by_router, by_in, by_out, by_token, by_token, by_token),
        out_specs=(by_token, by_in, by_out, by_router),
        check_vma=False,
    )
```

```python
import jax
import jax.numpy as jnp
from jax import lax
from jax.experimental import pallas as pl
from jax.experimental.pallas import tpu as pltpu
from jax.sharding import Mesh
from jax.sharding import PartitionSpec as P

CAP = 2
SPLIT = 2
META = 128
TILE = 256
SWAP = [(0, 1), (1, 0)]
BF = jnp.bfloat16
F32 = jnp.float32
VMEM = pl.BlockSpec(memory_space=pltpu.VMEM)
SMEM = pl.BlockSpec(memory_space=pltpu.SMEM)


def gelu_parts(pre_act):
    cubic_term = 0.044715 * pre_act * pre_act * pre_act
    tanh_value = jnp.tanh(0.7978845608028654 * (pre_act + cubic_term))
    gelu_value = 0.5 * pre_act * (1.0 + tanh_value)
    gelu_slope = 0.5 * (1.0 + tanh_value) + 0.5 * pre_act * (
        1.0 - tanh_value * tanh_value
    ) * 0.7978845608028654 * (1.0 + 3.0 * 0.044715 * pre_act * pre_act)
    return (gelu_value, gelu_slope)


def dot(a, b, dims):
    return lax.dot_general(a, b, (dims, ((), ())), preferred_element_type=F32)


def params():
    return pltpu.CompilerParams(vmem_limit_bytes=40 * 1024 * 1024)


def cost(flops, moved, special=0):
    return pl.CostEstimate(flops=flops, bytes_accessed=moved, transcendentals=special)


def struct(shape, dtype):
    return jax.ShapeDtypeStruct(shape, dtype)


def build_kernel(tok_ref, grad_ref, ids_ref, slot_ref, keep_ref, router_ref, out_ref):
    slots, width = tok_ref.shape
    part = router_ref.shape[1]
    ids = ids_ref[...]
    active = (keep_ref[...] == 1) & (ids < slots // CAP)
    code = jnp.where(active, ids * CAP + slot_ref[...], -1)
    slot_axis = lax.broadcasted_iota(jnp.int32, (slots, slots), 0)
    first = (slot_axis == code[0:1]).astype(F32)
    second = (slot_axis == code[1:2]).astype(F32)
    place = (first + second).astype(BF)
    out_ref[:, :width] = dot(place, tok_ref[...], ((1,), (0,))).astype(BF)
    out_ref[:, width + part + META :] = dot(place, grad_ref[...], ((1,), (0,))).astype(BF)
    wide_ids = ids.astype(F32)
    other = jnp.sum(first * wide_ids[1:2] + second * wide_ids[0:1], axis=1, keepdims=True)
    out_ref[:, width + part : width + part + META] = jnp.broadcast_to(other, (slots, META)).astype(
        BF
    )
    even = lax.broadcasted_iota(jnp.int32, (slots, part), 0) % CAP == 0
    router = router_ref[...].astype(F32)
    out_ref[:, width : width + part] = jnp.where(even, router[0:1], router[1:2]).astype(BF)


def unpack_kernel(place_ref, b0, b1, b2, b3, x_ref, router_ref, other_ref):
    slots, width = b0.shape[0], x_ref.shape[1]
    groups = 4
    part = width // groups
    for i, ref in enumerate((b0, b1, b2, b3)):
        x_ref[i * slots : (i + 1) * slots, :] = ref[:, :width]
        other_ref[i * slots : (i + 1) * slots, :] = ref[:, width + part : width + part + META]
        lane = pl.multiple_of((place_ref[0] + i) % groups * part, part)
        router_ref[:, pl.ds(lane, part)] = ref[:, width : width + part]


def up_kernel(x_ref, own_ref, sib_ref, hid_own, slope_own, hid_sib, slope_sib):
    x_rows = x_ref[...]
    for w_ref, hid_ref, slope_ref in ((own_ref, hid_own, slope_own), (sib_ref, hid_sib, slope_sib)):
        value, slope = gelu_parts(dot(x_rows, w_ref[...], ((1,), (0,))))
        hid_ref[...] = value.astype(BF)
        slope_ref[...] = slope


def gate_kernel(place_ref, x_ref, own_ref, sib_ref, other_ref, gate_ref, sign_ref):
    rows, half = x_ref.shape[0], own_ref.shape[0]
    core, own_column = place_ref[1], place_ref[2]
    other = other_ref[:, 0:1].astype(F32).astype(jnp.int32)
    pair = other // (CAP * SPLIT) * CAP + other % CAP
    other_column = jnp.where((other // CAP) % SPLIT == core, pair, pair + half)
    axis = lax.broadcasted_iota(jnp.int32, (rows, 2 * half), 1)
    sign = (axis == own_column).astype(F32) - (axis == other_column).astype(F32)
    x_rows = x_ref[...]
    gap = jnp.sum(
        dot(x_rows, own_ref[...], ((1,), (1,))) * sign[:, :half]
        + dot(x_rows, sib_ref[...], ((1,), (1,))) * sign[:, half:],
        axis=1,
        keepdims=True,
    )
    gate = jax.nn.sigmoid(gap)
    gate_ref[...] = jnp.broadcast_to(gate.astype(BF).astype(F32), gate_ref.shape)
    sign_ref[...] = gate * jax.nn.sigmoid(-gap) * sign


def back_kernel(
    d0, d1, d2, d3, gate_ref, sign_ref, x_ref, out_own, out_sib, hid_own, slope_own, hid_sib,
    slope_sib, pre_own, pre_sib, scaled_ref, logit_ref, router_ref, dy_ref, total_ref,
):
    step = pl.program_id(0)
    slots = d0.shape[0]

    @pl.when(step == 0)
    def _():
        total_ref[...] = jnp.zeros_like(total_ref)
        for i, ref in enumerate((d0, d1, d2, d3)):
            here = pl.ds(i * slots, slots)
            dy_ref[here, :] = ref[...]
            scaled_ref[here, :] = (gate_ref[here, 0:1] * ref[...].astype(F32)).astype(BF)

    dy_rows = dy_ref[...]
    gate = gate_ref[:, 0:1]
    for w_ref, hid_ref, slope_ref, pre_ref in (
        (out_own, hid_own, slope_own, pre_own),
        (out_sib, hid_sib, slope_sib, pre_sib),
    ):
        back_up = dot(dy_rows, w_ref[...], ((1,), (1,)))
        total_ref[...] += jnp.sum(back_up * hid_ref[...].astype(F32), axis=1, keepdims=True)
        pre_ref[...] = (gate * back_up * slope_ref[...]).astype(BF)

    @pl.when(step == pl.num_programs(0) - 1)
    def _():
        logit_grad = sign_ref[...] * total_ref[:, 0:1]
        logit_ref[...] = logit_grad.astype(BF)
        router_ref[...] = dot(logit_grad.T.astype(BF), x_ref[...], ((1,), (0,))).astype(BF)


def rows_kernel(pre_own, pre_sib, logit_ref, in_own, in_sib, router_own, router_sib, row_ref):
    half = router_own.shape[0]
    row_ref[...] = (
        dot(pre_own[...], in_own[...], ((1,), (1,)))
        + dot(pre_sib[...], in_sib[...], ((1,), (1,)))
        + dot(logit_ref[:, :half], router_own[...], ((1,), (0,)))
        + dot(logit_ref[:, half:], router_sib[...], ((1,), (0,)))
    ).astype(BF)


def pack_kernel(place_ref, row_ref, part_ref, recv_ref, o0, o1, o2, o3):
    slots, width = o0.shape[0], row_ref.shape[1]
    groups = 4
    part = width // groups
    for i, ref in enumerate((o0, o1, o2, o3)):
        lanes = pl.ds(pl.multiple_of((place_ref[0] + i) % groups * part, part), part)
        ref[:, :width] = row_ref[i * slots : (i + 1) * slots, :]
        ref[:, width:] = (
            part_ref[:slots, lanes].astype(F32) + recv_ref[:, lanes].astype(F32)
        ).astype(BF)


def shift_group(value, step):
    count = lax.axis_size("group")
    return lax.ppermute(value, "group", [(i, (i + step) % count) for i in range(count)])


def swap_cores(value):
    return lax.ppermute(value, "core", SWAP)


def call(kernel, out_shape, in_specs, cost_estimate):
    return pl.pallas_call(
        kernel,
        out_shape=out_shape,
        in_specs=in_specs,
        out_specs=jax.tree.map(lambda _: VMEM, out_shape),
        compiler_params=params(),
        cost_estimate=cost_estimate,
    )


def body(tokens, out_grad, w_router, w_in, w_out, expert_ids, slot_ids, keep_mask):
    chips = lax.axis_size("chip")
    groups = lax.axis_size("group")
    chip = lax.axis_index("chip")
    core = lax.axis_index("core")
    group = lax.axis_index("group")
    width = tokens.shape[1]
    hidden = w_in.shape[2]
    slot_count = chips * CAP
    row_count = slot_count * groups
    part = w_router.shape[0]
    w_in_own, w_out_own = w_in[0], w_out[0]
    w_in_sib, w_out_sib = swap_cores(w_in_own), swap_cores(w_out_own)
    pair = chip // (CAP * SPLIT) * CAP + chip % CAP
    own_column = jnp.where((chip // CAP) % SPLIT == core, pair, pair + slot_count)
    place = jnp.stack([group, core, own_column]).astype(jnp.int32)

    wide_x = width + part + META
    send = call(
        build_kernel,
        struct((slot_count, wide_x + width), BF),
        [VMEM] * 6,
        cost(4 * slot_count * slot_count * width, 4 * slot_count * width * 2),
    )(tokens, out_grad, expert_ids.T, slot_ids.T, keep_mask.T, w_router.T)

    def exchange(value):
        wide = value.shape[1]
        return lax.all_to_all(
            value.reshape(chips, CAP, wide), "chip", split_axis=0, concat_axis=0, tiled=True
        )

    def gather(value):
        return [value, shift_group(value, -1), shift_group(value, 2), shift_group(value, 1)]

    recv = exchange(send).reshape(slot_count, wide_x + width)
    x_blocks = gather(recv[:, :wide_x])
    dy_blocks = gather(recv[:, wide_x:])

    x_rows, router_own, other = call(
        unpack_kernel,
        (
            struct((row_count, width), BF),
            struct((slot_count, width), BF),
            struct((row_count, META), BF),
        ),
        [SMEM] + [VMEM] * 4,
        cost(0, row_count * width * 6),
    )(place, *x_blocks)
    router_sib = swap_cores(router_own)

    steps = hidden // TILE
    whole = lambda shape: pl.BlockSpec(shape, lambda i: (0,) * len(shape))
    tall = pl.BlockSpec((row_count, TILE), lambda i: (0, i))
    macs = row_count * width * hidden * 2
    hid_own, slope_own, hid_sib, slope_sib = pl.pallas_call(
        up_kernel,
        grid=(steps,),
        out_shape=(
            struct((row_count, hidden), BF),
            struct((row_count, hidden), F32),
            struct((row_count, hidden), BF),
            struct((row_count, hidden), F32),
        ),
        in_specs=[whole((row_count, width))] + [pl.BlockSpec((width, TILE), lambda i: (0, i))] * 2,
        out_specs=(tall,) * 4,
        compiler_params=params(),
        cost_estimate=cost(2 * macs, row_count * width * 12, 2 * row_count * hidden),
    )(x_rows, w_in_own, w_in_sib)

    gate, sign = call(
        gate_kernel,
        (struct((row_count, META), F32), struct((row_count, 2 * slot_count), F32)),
        [SMEM] + [VMEM] * 4,
        cost(4 * row_count * width * slot_count, row_count * width * 4),
    )(place, x_rows, router_own, router_sib, other)

    block = pl.BlockSpec((slot_count, width), lambda i: (0, 0))
    flat = pl.BlockSpec((TILE, width), lambda i: (i, 0))
    pre_own, pre_sib, scaled, logit_grad, router_part = pl.pallas_call(
        back_kernel,
        grid=(steps,),
        out_shape=(
            struct((row_count, hidden), BF),
            struct((row_count, hidden), BF),
            struct((row_count, width), BF),
            struct((row_count, 2 * slot_count), BF),
            struct((2 * slot_count, width), BF),
        ),
        in_specs=[block] * 4
        + [
            whole((row_count, META)),
            whole((row_count, 2 * slot_count)),
            whole((row_count, width)),
            flat,
            flat,
            tall,
            tall,
            tall,
            tall,
        ],
        out_specs=(
            tall,
            tall,
            whole((row_count, width)),
            whole((row_count, 2 * slot_count)),
            whole((2 * slot_count, width)),
        ),
        scratch_shapes=[pltpu.VMEM((row_count, width), BF), pltpu.VMEM((row_count, META), F32)],
        compiler_params=params(),
        cost_estimate=cost(2 * macs, row_count * width * 16),
    )(
        *dy_blocks, gate, sign, x_rows, w_out_own, w_out_sib, hid_own, slope_own, hid_sib, slope_sib
    )
    router_recv = swap_cores(router_part[slot_count:])

    columns = pl.BlockSpec((slot_count, TILE), lambda i: (0, i))
    row_part = pl.pallas_call(
        rows_kernel,
        grid=(width // TILE,),
        out_shape=struct((row_count, width), BF),
        in_specs=[
            whole((row_count, hidden)),
            whole((row_count, hidden)),
            whole((row_count, 2 * slot_count)),
            pl.BlockSpec((TILE, hidden), lambda i: (i, 0)),
            pl.BlockSpec((TILE, hidden), lambda i: (i, 0)),
            columns,
            columns,
        ],
        out_specs=tall,
        compiler_params=params(),
        cost_estimate=cost(2 * macs, row_count * width * 8),
    )(pre_own, pre_sib, logit_grad, w_in_own, w_in_sib, router_own, router_sib)

    back = call(
        pack_kernel,
        (struct((slot_count, width + part), BF),) * groups,
        [SMEM] + [VMEM] * 3,
        cost(0, row_count * width * 4),
    )(place, row_part, router_part, router_recv)
    total = (
        back[0].astype(F32)
        + shift_group(back[1], 1).astype(F32)
        + shift_group(back[2], 2).astype(F32)
        + shift_group(back[3], -1).astype(F32)
    ).astype(BF)
    home = exchange(total)
    rows_home = home[:, :, :width].reshape(slot_count, width)
    active = (keep_mask == 1) & (expert_ids < chips)
    slot_code = jnp.where(active, expert_ids * CAP + slot_ids, -1)
    slot_axis = jnp.arange(slot_count, dtype=jnp.int32)
    pick = (slot_axis == slot_code[:, 0:1]) | (slot_axis == slot_code[:, 1:2])
    in_grad = dot(pick.astype(BF), rows_home, ((1,), (0,))).astype(BF)
    router_grad = jnp.sum(home[:, :, width:].astype(F32), axis=0).T

    in_sib = swap_cores(dot(x_rows, pre_sib, ((0,), (0,))).astype(BF))
    out_sib = swap_cores(dot(hid_sib, scaled, ((0,), (0,))).astype(BF))
    w_in_grad = (dot(x_rows, pre_own, ((0,), (0,))) + in_sib.astype(F32)).astype(BF)[None]
    w_out_grad = (dot(hid_own, scaled, ((0,), (0,))) + out_sib.astype(F32)).astype(BF)[None]
    return (in_grad, w_in_grad, w_out_grad, router_grad)


def solution(mesh):
    experts, groups = mesh.devices.shape
    cut = Mesh(
        mesh.devices.reshape(experts // SPLIT, SPLIT, groups), ("chip", "core", "group")
    )
    by_token = P(("chip", "core", "group"), None)
    by_router = P("group", ("chip", "core"))
    by_in = P(("chip", "core"), None, "group")
    by_out = P(("chip", "core"), "group", None)
    return jax.shard_map(
        body,
        mesh=cut,
        in_specs=(by_token, by_token, by_router, by_in, by_out, by_token, by_token, by_token),
        out_specs=(by_token, by_in, by_out, by_router),
        check_vma=False,
    )
```

```python
import functools

import jax
import jax.numpy as jnp
from jax import lax
from jax.experimental import pallas as pl
from jax.experimental.pallas import tpu as pltpu
from jax.sharding import Mesh
from jax.sharding import PartitionSpec as P

CAP = 2
SPLIT = 2
META = 128
TILE = 256
ORDER = (0, 1, 3, 2)
SWAP = [(0, 1), (1, 0)]
BF = jnp.bfloat16
F32 = jnp.float32
VMEM = pl.BlockSpec(memory_space=pltpu.VMEM)
SMEM = pl.BlockSpec(memory_space=pltpu.SMEM)


def gelu_parts(pre_act):
    cubic_term = 0.044715 * pre_act * pre_act * pre_act
    tanh_value = jnp.tanh(0.7978845608028654 * (pre_act + cubic_term))
    gelu_value = 0.5 * pre_act * (1.0 + tanh_value)
    gelu_slope = 0.5 * (1.0 + tanh_value) + 0.5 * pre_act * (
        1.0 - tanh_value * tanh_value
    ) * 0.7978845608028654 * (1.0 + 3.0 * 0.044715 * pre_act * pre_act)
    return (gelu_value, gelu_slope)


def dot(a, b, dims):
    return lax.dot_general(a, b, (dims, ((), ())), preferred_element_type=F32)


def params():
    return pltpu.CompilerParams(vmem_limit_bytes=40 * 1024 * 1024)


def cost(flops, moved, special=0):
    return pl.CostEstimate(flops=flops, bytes_accessed=moved, transcendentals=special)


def struct(shape, dtype):
    return jax.ShapeDtypeStruct(shape, dtype)


def build_kernel(tok_ref, grad_ref, ids_ref, slot_ref, keep_ref, router_ref, out_ref):
    slots, width = tok_ref.shape
    part = router_ref.shape[1]
    ids = ids_ref[...]
    active = (keep_ref[...] == 1) & (ids < slots // CAP)
    code = jnp.where(active, ids * CAP + slot_ref[...], -1)
    slot_axis = lax.broadcasted_iota(jnp.int32, (slots, slots), 0)
    first = (slot_axis == code[0:1]).astype(F32)
    second = (slot_axis == code[1:2]).astype(F32)
    place = (first + second).astype(BF)
    out_ref[:, :width] = dot(place, tok_ref[...], ((1,), (0,))).astype(BF)
    out_ref[:, width + part + META :] = dot(place, grad_ref[...], ((1,), (0,))).astype(BF)
    wide_ids = ids.astype(F32)
    other = jnp.sum(first * wide_ids[1:2] + second * wide_ids[0:1], axis=1, keepdims=True)
    out_ref[:, width + part : width + part + META] = jnp.broadcast_to(other, (slots, META)).astype(
        BF
    )
    even = lax.broadcasted_iota(jnp.int32, (slots, part), 0) % CAP == 0
    router = router_ref[...].astype(F32)
    out_ref[:, width : width + part] = jnp.where(even, router[0:1], router[1:2]).astype(BF)


def unpack_kernel(place_ref, b0, b1, b2, b3, x_ref, router_ref):
    slots, width = b0.shape[0], x_ref.shape[1]
    groups = len(ORDER)
    part = width // groups
    for i, ref in enumerate((b0, b1, b2, b3)):
        x_ref[i * slots : (i + 1) * slots, :] = ref[:, :width]
        lane = pl.multiple_of((place_ref[0] + ORDER[i]) % groups * part, part)
        router_ref[:, pl.ds(lane, part)] = ref[:, width : width + part]


def expert_kernel(count, *refs):
    blocks, rest = refs[:count], refs[count:]
    in_own, in_sib, out_own, out_sib = rest[:4]
    hid_own, hid_sib, slope_own, slope_sib, total_ref, x_ref, dy_ref = rest[4:]
    slots, width = blocks[0].shape[0], x_ref.shape[1]

    @pl.when(pl.program_id(0) == 0)
    def _():
        total_ref[...] = jnp.zeros_like(total_ref)
        for i, ref in enumerate(blocks):
            x_ref[i * slots : (i + 1) * slots, :] = ref[:, :width]
            dy_ref[i * slots : (i + 1) * slots, :] = ref[:, ref.shape[1] - width :]

    x_rows, dy_rows = x_ref[...], dy_ref[...]
    for w_in, w_out, hid_ref, slope_ref in (
        (in_own, out_own, hid_own, slope_own),
        (in_sib, out_sib, hid_sib, slope_sib),
    ):
        value, slope = gelu_parts(dot(x_rows, w_in[...], ((1,), (0,))))
        back_up = dot(dy_rows, w_out[...], ((1,), (1,)))
        hid_ref[...] = value.astype(BF)
        slope_ref[...] = back_up * slope
        total_ref[...] += jnp.sum(back_up * value, axis=1, keepdims=True)


def gate_kernel(
    place_ref, x_ref, own_ref, sib_ref, b0, b1, b2, b3, near_own, near_sib, far_own, far_sib,
    near_total, far_total, pre_own, pre_sib, scaled_ref, logit_ref, router_ref,
):
    rows, width = x_ref.shape
    half, slots = own_ref.shape[0], b0.shape[0]
    core, own_column = place_ref[1], place_ref[2]
    part = width // len(ORDER)
    meta = pl.ds(width + part, META)
    blocks = (b0, b1, b2, b3)
    other = jnp.concatenate([ref[:, meta] for ref in blocks], axis=0)[:, 0:1]
    other = other.astype(F32).astype(jnp.int32)
    pair = other // (CAP * SPLIT) * CAP + other % CAP
    other_column = jnp.where((other // CAP) % SPLIT == core, pair, pair + half)
    axis = lax.broadcasted_iota(jnp.int32, (rows, 2 * half), 1)
    sign = (axis == own_column).astype(F32) - (axis == other_column).astype(F32)
    x_rows = x_ref[...]
    gap = jnp.sum(
        dot(x_rows, own_ref[...], ((1,), (1,))) * sign[:, :half]
        + dot(x_rows, sib_ref[...], ((1,), (1,))) * sign[:, half:],
        axis=1,
        keepdims=True,
    )
    combine = jax.nn.sigmoid(gap)
    gate = combine.astype(BF).astype(F32)
    near = near_own.shape[0]
    for near_ref, far_ref, pre_ref in (
        (near_own, far_own, pre_own),
        (near_sib, far_sib, pre_sib),
    ):
        pre_ref[:near, :] = (gate[:near] * near_ref[...]).astype(BF)
        pre_ref[near:, :] = (gate[near:] * far_ref[...]).astype(BF)
    for i, ref in enumerate(blocks):
        here = slice(i * slots, (i + 1) * slots)
        dy_rows = ref[:, ref.shape[1] - width :].astype(F32)
        scaled_ref[here, :] = (gate[here] * dy_rows).astype(BF)
    total = jnp.concatenate([near_total[:, 0:1], far_total[:, 0:1]], axis=0)
    logit_grad = combine * jax.nn.sigmoid(-gap) * total * sign
    logit_ref[...] = logit_grad.astype(BF)
    router_ref[...] = dot(logit_grad.T.astype(BF), x_rows, ((1,), (0,))).astype(BF)


def rows_kernel(pre_own, pre_sib, logit_ref, in_own, in_sib, router_own, router_sib, row_ref):
    half = router_own.shape[0]
    row_ref[...] = (
        dot(pre_own[...], in_own[...], ((1,), (1,)))
        + dot(pre_sib[...], in_sib[...], ((1,), (1,)))
        + dot(logit_ref[:, :half], router_own[...], ((1,), (0,)))
        + dot(logit_ref[:, half:], router_sib[...], ((1,), (0,)))
    ).astype(BF)


def pack_kernel(place_ref, row_ref, part_ref, recv_ref, out_ref):
    groups, slots = out_ref.shape[0], out_ref.shape[1]
    width = row_ref.shape[1]
    part = width // groups
    for i in range(groups):
        target = (place_ref[0] + ORDER[i]) % groups
        lanes = pl.ds(pl.multiple_of(target * part, part), part)
        out_ref[target, :, :width] = row_ref[i * slots : (i + 1) * slots, :]
        out_ref[target, :, width:] = (
            part_ref[:slots, lanes].astype(F32) + recv_ref[:, lanes].astype(F32)
        ).astype(BF)


def shift_group(value, step):
    count = lax.axis_size("group")
    return lax.ppermute(value, "group", [(i, (i + step) % count) for i in range(count)])


def swap_cores(value):
    return lax.ppermute(value, "core", SWAP)


def call(kernel, out_shape, in_specs, cost_estimate):
    return pl.pallas_call(
        kernel,
        out_shape=out_shape,
        in_specs=in_specs,
        out_specs=jax.tree.map(lambda _: VMEM, out_shape),
        compiler_params=params(),
        cost_estimate=cost_estimate,
    )


def body(tokens, out_grad, w_router, w_in, w_out, expert_ids, slot_ids, keep_mask):
    chips = lax.axis_size("chip")
    groups = lax.axis_size("group")
    chip = lax.axis_index("chip")
    core = lax.axis_index("core")
    group = lax.axis_index("group")
    width = tokens.shape[1]
    hidden = w_in.shape[2]
    slot_count = chips * CAP
    row_count = slot_count * groups
    part = w_router.shape[0]
    w_in_own, w_out_own = w_in[0], w_out[0]
    w_in_sib, w_out_sib = swap_cores(w_in_own), swap_cores(w_out_own)
    pair = chip // (CAP * SPLIT) * CAP + chip % CAP
    own_column = jnp.where((chip // CAP) % SPLIT == core, pair, pair + slot_count)
    place = jnp.stack([group, core, own_column]).astype(jnp.int32)

    wide_x = width + part + META
    whole = lambda shape: pl.BlockSpec(shape, lambda i: (0,) * len(shape))
    operands = (tokens, out_grad, expert_ids.T, slot_ids.T, keep_mask.T, w_router.T)
    send = pl.pallas_call(
        build_kernel,
        grid=(1,),
        out_shape=struct((slot_count, wide_x + width), BF),
        in_specs=[whole(o.shape) for o in operands],
        out_specs=whole((slot_count, wide_x + width)),
        compiler_params=params(),
        cost_estimate=cost(4 * slot_count * slot_count * width, 4 * slot_count * width * 2),
    )(*operands)

    def exchange(value):
        wide = value.shape[1]
        return lax.all_to_all(
            value.reshape(chips, CAP, wide), "chip", split_axis=0, concat_axis=0, tiled=True
        )

    recv = exchange(send).reshape(slot_count, wide_x + width)
    blocks = [recv, shift_group(recv, -1), shift_group(recv, 1), shift_group(recv, 2)]

    steps = hidden // TILE

    def expert(pieces):
        rows = len(pieces) * slot_count
        tall = pl.BlockSpec((rows, TILE), lambda i: (0, i))
        return pl.pallas_call(
            functools.partial(expert_kernel, len(pieces)),
            grid=(steps,),
            out_shape=(struct((rows, hidden), BF),) * 2
            + (struct((rows, hidden), F32),) * 2
            + (struct((rows, META), F32),),
            in_specs=[whole(p.shape) for p in pieces]
            + [pl.BlockSpec((width, TILE), lambda i: (0, i))] * 2
            + [pl.BlockSpec((TILE, width), lambda i: (i, 0))] * 2,
            out_specs=(tall,) * 4 + (whole((rows, META)),),
            scratch_shapes=[pltpu.VMEM((rows, width), BF)] * 2,
            compiler_params=params(),
            cost_estimate=cost(4 * rows * width * hidden * 2, rows * width * 16),
        )(*pieces, w_in_own, w_in_sib, w_out_own, w_out_sib)

    near_hid_own, near_hid_sib, near_own, near_sib, near_total = expert(blocks[:3])
    blocks[3], near_total = lax.optimization_barrier((blocks[3], near_total))
    far_hid_own, far_hid_sib, far_own, far_sib, far_total = expert(blocks[3:])
    x_rows, router_own = call(
        unpack_kernel,
        (struct((row_count, width), BF), struct((slot_count, width), BF)),
        [SMEM] + [VMEM] * 4,
        cost(0, row_count * width * 4),
    )(place, *blocks)
    router_sib = swap_cores(router_own)
    pre_own, pre_sib, scaled, logit_grad, router_part = call(
        gate_kernel,
        (
            struct((row_count, hidden), BF),
            struct((row_count, hidden), BF),
            struct((row_count, width), BF),
            struct((row_count, 2 * slot_count), BF),
            struct((2 * slot_count, width), BF),
        ),
        [SMEM] + [VMEM] * 13,
        cost(8 * row_count * width * slot_count, row_count * width * 12),
    )(
        place, x_rows, router_own, router_sib, *blocks, near_own, near_sib, far_own, far_sib,
        near_total, far_total,
    )
    router_recv = swap_cores(router_part[slot_count:])

    macs = row_count * width * hidden * 2
    columns = pl.BlockSpec((slot_count, TILE), lambda i: (0, i))
    row_part = pl.pallas_call(
        rows_kernel,
        grid=(width // TILE,),
        out_shape=struct((row_count, width), BF),
        in_specs=[
            whole((row_count, hidden)),
            whole((row_count, hidden)),
            whole((row_count, 2 * slot_count)),
            pl.BlockSpec((TILE, hidden), lambda i: (i, 0)),
            pl.BlockSpec((TILE, hidden), lambda i: (i, 0)),
            columns,
            columns,
        ],
        out_specs=pl.BlockSpec((row_count, TILE), lambda i: (0, i)),
        compiler_params=params(),
        cost_estimate=cost(2 * macs, row_count * width * 8),
    )(pre_own, pre_sib, logit_grad, w_in_own, w_in_sib, router_own, router_sib)

    back = call(
        pack_kernel,
        struct((groups, slot_count, width + part), BF),
        [SMEM] + [VMEM] * 3,
        cost(0, row_count * width * 4),
    )(place, row_part, router_part, router_recv)
    back, x_rows, pre_sib, scaled = lax.optimization_barrier((back, x_rows, pre_sib, scaled))
    total = jnp.sum(
        lax.all_to_all(back, "group", split_axis=0, concat_axis=0, tiled=True).astype(F32), axis=0
    ).astype(BF)
    total, x_own, pre_own, scaled_own = lax.optimization_barrier((total, x_rows, pre_own, scaled))
    hid_own = jnp.concatenate([near_hid_own, far_hid_own], axis=0)
    hid_sib = jnp.concatenate([near_hid_sib, far_hid_sib], axis=0)
    home = exchange(total)
    rows_home = home[:, :, :width].reshape(slot_count, width)
    active = (keep_mask == 1) & (expert_ids < chips)
    slot_code = jnp.where(active, expert_ids * CAP + slot_ids, -1)
    slot_axis = jnp.arange(slot_count, dtype=jnp.int32)
    pick = (slot_axis == slot_code[:, 0:1]) | (slot_axis == slot_code[:, 1:2])
    in_grad = dot(pick.astype(BF), rows_home, ((1,), (0,))).astype(BF)
    router_grad = jnp.sum(home[:, :, width:].astype(F32), axis=0).T

    in_sib = swap_cores(dot(x_rows, pre_sib, ((0,), (0,))).astype(BF))
    out_sib = swap_cores(dot(hid_sib, scaled, ((0,), (0,))).astype(BF))
    w_in_grad = (dot(x_own, pre_own, ((0,), (0,))) + in_sib.astype(F32)).astype(BF)[None]
    w_out_grad = (dot(hid_own, scaled_own, ((0,), (0,))) + out_sib.astype(F32)).astype(BF)[None]
    return (in_grad, w_in_grad, w_out_grad, router_grad)


def solution(mesh):
    experts, groups = mesh.devices.shape
    cut = Mesh(
        mesh.devices.reshape(experts // SPLIT, SPLIT, groups), ("chip", "core", "group")
    )
    by_token = P(("chip", "core", "group"), None)
    by_router = P("group", ("chip", "core"))
    by_in = P(("chip", "core"), None, "group")
    by_out = P(("chip", "core"), "group", None)
    return jax.shard_map(
        body,
        mesh=cut,
        in_specs=(by_token, by_token, by_router, by_in, by_out, by_token, by_token, by_token),
        out_specs=(by_token, by_in, by_out, by_router),
        check_vma=False,
    )
```

```python
import functools

import jax
import jax.numpy as jnp
from jax import lax
from jax.experimental import pallas as pl
from jax.experimental.pallas import tpu as pltpu
from jax.sharding import Mesh
from jax.sharding import PartitionSpec as P

CAP = 2
SPLIT = 2
META = 128
TILE = 256
SWAP = [(0, 1), (1, 0)]
BF = jnp.bfloat16
F32 = jnp.float32
VMEM = pl.BlockSpec(memory_space=pltpu.VMEM)
SMEM = pl.BlockSpec(memory_space=pltpu.SMEM)


def gelu_parts(pre_act):
    cubic_term = 0.044715 * pre_act * pre_act * pre_act
    tanh_value = jnp.tanh(0.7978845608028654 * (pre_act + cubic_term))
    gelu_value = 0.5 * pre_act * (1.0 + tanh_value)
    gelu_slope = 0.5 * (1.0 + tanh_value) + 0.5 * pre_act * (
        1.0 - tanh_value * tanh_value
    ) * 0.7978845608028654 * (1.0 + 3.0 * 0.044715 * pre_act * pre_act)
    return (gelu_value, gelu_slope)


def dot(a, b, dims):
    return lax.dot_general(a, b, (dims, ((), ())), preferred_element_type=F32)


def params():
    return pltpu.CompilerParams(vmem_limit_bytes=40 * 1024 * 1024)


def cost(flops, moved, special=0):
    return pl.CostEstimate(flops=flops, bytes_accessed=moved, transcendentals=special)


def struct(shape, dtype):
    return jax.ShapeDtypeStruct(shape, dtype)


def build_kernel(*refs):
    sources, out_ref, held, sem = refs[:6], refs[6], refs[7:13], refs[13]
    copies = [pltpu.make_async_copy(s, h, sem.at[i]) for i, (s, h) in enumerate(zip(sources, held))]
    for copy in copies:
        copy.start()
    for copy in copies[2:]:
        copy.wait()
    tok_ref, grad_ref, ids_ref, slot_ref, keep_ref, router_ref = held
    slots, width = tok_ref.shape
    part = router_ref.shape[1]
    ids = ids_ref[...]
    active = (keep_ref[...] == 1) & (ids < slots // CAP)
    code = jnp.where(active, ids * CAP + slot_ref[...], -1)
    slot_axis = lax.broadcasted_iota(jnp.int32, (slots, slots), 0)
    first = (slot_axis == code[0:1]).astype(F32)
    second = (slot_axis == code[1:2]).astype(F32)
    place = (first + second).astype(BF)
    wide_ids = ids.astype(F32)
    other = jnp.sum(first * wide_ids[1:2] + second * wide_ids[0:1], axis=1, keepdims=True)
    other = jnp.broadcast_to(other, (slots, META)).astype(BF)
    out_ref[:, 2 * width : 2 * width + META] = other
    even = lax.broadcasted_iota(jnp.int32, (slots, part), 0) % CAP == 0
    router = router_ref[...].astype(F32)
    out_ref[:, 2 * width + META :] = jnp.where(even, router[0:1], router[1:2]).astype(BF)
    copies[0].wait()
    out_ref[:, :width] = dot(place, tok_ref[...], ((1,), (0,))).astype(BF)
    copies[1].wait()
    out_ref[:, width : 2 * width] = dot(place, grad_ref[...], ((1,), (0,))).astype(BF)


def router_kernel(place_ref, r0, r1, r2, r3, router_ref):
    pieces = (r0, r1, r2, r3)
    part = r0.shape[1]
    for i, ref in enumerate(pieces):
        lane = pl.multiple_of((place_ref[0] + i) % len(pieces) * part, part)
        router_ref[:, pl.ds(lane, part)] = ref[...]


def expert_kernel(count, sets, *refs):
    blocks, weights, outs = refs[:count], refs[count : count + 2 * sets], refs[count + 2 * sets :]
    w_ins, w_outs = weights[:sets], weights[sets:]
    hid_own, hid_sib, total_ref = outs[:3]
    slopes, (x_ref, dy_ref) = outs[3 : 3 + sets], outs[3 + sets :]
    slots, width = blocks[0].shape[0], x_ref.shape[1]

    @pl.when(pl.program_id(0) == 0)
    def _():
        total_ref[...] = jnp.zeros_like(total_ref)
        for i, ref in enumerate(blocks):
            x_ref[i * slots : (i + 1) * slots, :] = ref[:, :width]
            dy_ref[i * slots : (i + 1) * slots, :] = ref[:, width : 2 * width]

    x_rows, dy_rows = x_ref[...], dy_ref[...]
    hids = (hid_own, hid_sib) + (None,) * (sets - 2)
    for w_in, w_out, hid_ref, slope_ref in zip(w_ins, w_outs, hids, slopes):
        value, slope = gelu_parts(dot(x_rows, w_in[...], ((1,), (0,))))
        back_up = dot(dy_rows, w_out[...], ((1,), (1,)))
        if hid_ref is not None:
            hid_ref[...] = value.astype(BF)
        slope_ref[...] = back_up * slope
        total_ref[...] += jnp.sum(back_up * value, axis=1, keepdims=True)


def gates_of(place_ref, own_ref, sib_ref, blocks):
    half, width = own_ref.shape
    core, own_column = place_ref[1], place_ref[2]
    other = jnp.concatenate([ref[:, 2 * width :] for ref in blocks], axis=0)[:, 0:1]
    other = other.astype(F32).astype(jnp.int32)
    pair = other // (CAP * SPLIT) * CAP + other % CAP
    other_column = jnp.where((other // CAP) % SPLIT == core, pair, pair + half)
    axis = lax.broadcasted_iota(jnp.int32, (other.shape[0], 2 * half), 1)
    sign = (axis == own_column).astype(F32) - (axis == other_column).astype(F32)
    x_rows = jnp.concatenate([ref[:, :width] for ref in blocks], axis=0)
    gap = jnp.sum(
        dot(x_rows, own_ref[...], ((1,), (1,))) * sign[:, :half]
        + dot(x_rows, sib_ref[...], ((1,), (1,))) * sign[:, half:],
        axis=1,
        keepdims=True,
    )
    combine = jax.nn.sigmoid(gap)
    return x_rows, sign, combine, combine * jax.nn.sigmoid(-gap)


def scale_rows(gate, blocks, scaled_ref):
    slots, width = blocks[0].shape[0], scaled_ref.shape[1]
    for i, ref in enumerate(blocks):
        here = slice(i * slots, (i + 1) * slots)
        dy_rows = ref[:, width : 2 * width].astype(F32)
        scaled_ref[here, :] = (gate[here] * dy_rows).astype(BF)


def gate_kernel(sets, place_ref, own_ref, sib_ref, b0, b1, near_total, far_total, *refs):
    nears, fars, pres = refs[:sets], refs[sets : 2 * sets], refs[2 * sets : 3 * sets]
    scaled_ref, logit_ref, router_ref = refs[3 * sets :]
    blocks = (b0, b1)
    x_rows, sign, combine, cross = gates_of(place_ref, own_ref, sib_ref, blocks)
    gate = combine.astype(BF).astype(F32)
    slots = b0.shape[0]
    for near_ref, far_ref, pre_ref in zip(nears, fars, pres):
        pre_ref[:slots, :] = (gate[:slots] * near_ref[...]).astype(BF)
        pre_ref[slots:, :] = (gate[slots:] * far_ref[...]).astype(BF)
    total = jnp.concatenate([near_total[:, 0:1], far_total[:, 0:1]], axis=0)
    logit_grad = cross * total * sign
    logit_ref[...] = logit_grad.astype(BF)
    router_ref[...] = dot(logit_grad.T.astype(BF), x_rows, ((1,), (0,))).astype(BF)
    scale_rows(gate, blocks, scaled_ref)


def late_kernel(place_ref, own_ref, sib_ref, b0, b1, own, sib, pre_own, pre_sib, scaled_ref):
    blocks = (b0, b1)
    _, _, combine, _ = gates_of(place_ref, own_ref, sib_ref, blocks)
    gate = combine.astype(BF).astype(F32)
    pre_own[...] = (gate * own[...]).astype(BF)
    pre_sib[...] = (gate * sib[...]).astype(BF)
    scale_rows(gate, blocks, scaled_ref)


def rows_kernel(sets, *refs):
    pres, w_ins = refs[:sets], refs[sets : 2 * sets]
    logit_ref, router_own, router_sib, row_ref = refs[2 * sets :]
    half = router_own.shape[0]
    rows = dot(logit_ref[:, :half], router_own[...], ((1,), (0,)))
    rows += dot(logit_ref[:, half:], router_sib[...], ((1,), (0,)))
    for pre_ref, w_in in zip(pres, w_ins):
        rows += dot(pre_ref[...], w_in[...], ((1,), (1,)))
    row_ref[...] = rows.astype(BF)


def pack_kernel(place_ref, row_ref, part_ref, recv_ref, keep_ref, far_ref, up_ref, down_ref):
    slots, part = up_ref.shape
    width = row_ref.shape[1]
    groups = width // part
    keep_ref[:, :width] = row_ref[:slots, :]
    far_ref[:, :width] = row_ref[slots:, :]
    for step, ref, at in ((0, keep_ref, width), (2, far_ref, width), (1, up_ref, 0), (3, down_ref, 0)):
        lanes = pl.ds(pl.multiple_of((place_ref[0] + step) % groups * part, part), part)
        ref[:, at : at + part] = (
            part_ref[:slots, lanes].astype(F32) + recv_ref[:, lanes].astype(F32)
        ).astype(BF)


def add_kernel(keep_ref, far_ref, up_ref, down_ref, out_ref):
    width = keep_ref.shape[1] - up_ref.shape[1]
    total = keep_ref[...].astype(F32) + far_ref[...].astype(F32)
    out_ref[:, :width] = total[:, :width].astype(BF)
    side = up_ref[...].astype(F32) + down_ref[...].astype(F32)
    out_ref[:, width:] = (total[:, width:] + side).astype(BF)


def shift_group(value, step):
    count = lax.axis_size("group")
    return lax.ppermute(value, "group", [(i, (i + step) % count) for i in range(count)])


def pair_groups(value):
    count = lax.axis_size("group")
    return lax.ppermute(value, "group", [(i, i ^ 1) for i in range(count)])


def swap_cores(value):
    return lax.ppermute(value, "core", SWAP)


def call(kernel, out_shape, in_specs, cost_estimate):
    return pl.pallas_call(
        kernel,
        out_shape=out_shape,
        in_specs=in_specs,
        out_specs=jax.tree.map(lambda _: VMEM, out_shape),
        compiler_params=params(),
        cost_estimate=cost_estimate,
    )


def body(tokens, out_grad, w_router, w_in, w_out, expert_ids, slot_ids, keep_mask):
    chips = lax.axis_size("chip")
    groups = lax.axis_size("group")
    chip = lax.axis_index("chip")
    core = lax.axis_index("core")
    group = lax.axis_index("group")
    width = tokens.shape[1]
    hidden = w_in.shape[2]
    slot_count = chips * CAP
    part = w_router.shape[0]
    pair = chip // (CAP * SPLIT) * CAP + chip % CAP
    own_column = jnp.where((chip // CAP) % SPLIT == core, pair, pair + slot_count)
    place = jnp.stack([group, core, own_column]).astype(jnp.int32)

    row_wide = 2 * width + META
    operands = (tokens, out_grad, expert_ids.T, slot_ids.T, keep_mask.T, w_router.T)
    send = pl.pallas_call(
        build_kernel,
        out_shape=struct((slot_count, row_wide + part), BF),
        in_specs=[pl.BlockSpec(memory_space=pl.ANY)] * len(operands),
        out_specs=VMEM,
        scratch_shapes=[pltpu.VMEM(o.shape, o.dtype) for o in operands]
        + [pltpu.SemaphoreType.DMA((len(operands),))],
        compiler_params=pltpu.CompilerParams(vmem_limit_bytes=56 * 1024 * 1024),
        cost_estimate=cost(4 * slot_count * slot_count * width, 4 * slot_count * width * 2),
    )(*operands)

    def exchange(value):
        return lax.all_to_all(value, "chip", split_axis=0, concat_axis=0, tiled=True)

    send, *own = lax.optimization_barrier((send, w_in[0], w_out[0]))
    sib = [swap_cores(w) for w in own]
    pair_own = [pair_groups(w) for w in own]
    pair_sib = [swap_cores(w) for w in pair_own]
    shards = [own, sib, pair_own, pair_sib]
    recv, shards = lax.optimization_barrier((exchange(send.reshape(chips, CAP, row_wide + part)), shards))
    w_ins, w_outs = [s[0] for s in shards], [s[1] for s in shards]
    recv = recv.reshape(slot_count, row_wide + part)
    own_rows = recv[:, :row_wide]
    far_rows = shift_group(own_rows, 2)
    piece = recv[:, row_wide:]
    router_own = call(
        router_kernel,
        struct((slot_count, width), BF),
        [SMEM] + [VMEM] * 4,
        cost(0, slot_count * width * 4),
    )(place, piece, shift_group(piece, -1), shift_group(piece, 2), shift_group(piece, 1))
    router_sib = swap_cores(router_own)

    steps = hidden // TILE
    whole = lambda shape: pl.BlockSpec(shape, lambda i: (0,) * len(shape))

    def expert(pieces, sets):
        rows = len(pieces) * slot_count
        tall = pl.BlockSpec((rows, TILE), lambda i: (0, i))
        return pl.pallas_call(
            functools.partial(expert_kernel, len(pieces), sets),
            grid=(steps,),
            out_shape=(struct((rows, hidden), BF),) * 2
            + (struct((rows, META), F32),)
            + (struct((rows, hidden), F32),) * sets,
            in_specs=[whole(p.shape) for p in pieces]
            + [pl.BlockSpec((width, TILE), lambda i: (0, i))] * sets
            + [pl.BlockSpec((TILE, width), lambda i: (i, 0))] * sets,
            out_specs=(tall,) * 2 + (whole((rows, META)),) + (tall,) * sets,
            scratch_shapes=[pltpu.VMEM((rows, width), BF)] * 2,
            compiler_params=params(),
            cost_estimate=cost(4 * rows * width * hidden * sets, rows * width * 8 * sets),
        )(*pieces, *w_ins[:sets], *w_outs[:sets])

    near_hid_own, near_hid_sib, near_total, *nears = expert([own_rows], 4)
    far_rows, near_total = lax.optimization_barrier((far_rows, near_total))
    far_hid_own, far_hid_sib, far_total, *fars = expert([far_rows], 4)
    work_rows = 2 * slot_count
    *pres, scaled, logit_grad, router_part = call(
        functools.partial(gate_kernel, 4),
        (struct((work_rows, hidden), BF),) * 4
        + (
            struct((work_rows, width), BF),
            struct((work_rows, 2 * slot_count), BF),
            struct((2 * slot_count, width), BF),
        ),
        [SMEM] + [VMEM] * 14,
        cost(8 * work_rows * width * slot_count, work_rows * width * 20),
    )(place, router_own, router_sib, own_rows, far_rows, near_total, far_total, *nears, *fars)
    router_recv = swap_cores(router_part[slot_count:])

    columns = pl.BlockSpec((slot_count, TILE), lambda i: (0, i))
    row_part = pl.pallas_call(
        functools.partial(rows_kernel, 4),
        grid=(width // TILE,),
        out_shape=struct((work_rows, width), BF),
        in_specs=[whole((work_rows, hidden))] * 4
        + [pl.BlockSpec((TILE, hidden), lambda i: (i, 0))] * 4
        + [whole((work_rows, 2 * slot_count)), columns, columns],
        out_specs=pl.BlockSpec((work_rows, TILE), lambda i: (0, i)),
        compiler_params=params(),
        cost_estimate=cost(8 * work_rows * width * hidden, work_rows * width * 16),
    )(*pres, *w_ins, logit_grad, router_own, router_sib)
    keep, far_part, up_part, down_part = call(
        pack_kernel,
        (struct((slot_count, width + part), BF),) * 2 + (struct((slot_count, part), BF),) * 2,
        [SMEM] + [VMEM] * 3,
        cost(0, work_rows * width * 4),
    )(place, row_part, router_part, router_recv)
    far_part = shift_group(far_part, 2)
    up_part = shift_group(up_part, 1)
    down_part = shift_group(down_part, -1)
    total = call(
        add_kernel, struct((slot_count, width + part), BF), [VMEM] * 4, cost(0, work_rows * width * 4)
    )(keep, far_part, up_part, down_part)
    total, late_source = lax.optimization_barrier((total.reshape(chips, CAP, width + part), own_rows))
    home = exchange(total)
    late_rows = [shift_group(late_source, -1), shift_group(late_source, 1)]
    late_hid_own, late_hid_sib, _, *lates = expert(late_rows, 2)
    late_own, late_sib, late_scaled = call(
        late_kernel,
        (struct((work_rows, hidden), BF),) * 2 + (struct((work_rows, width), BF),),
        [SMEM] + [VMEM] * 6,
        cost(4 * work_rows * width * slot_count, work_rows * width * 12),
    )(place, router_own, router_sib, *late_rows, *lates)
    x_rows = jnp.concatenate([r[:, :width] for r in (own_rows, far_rows, *late_rows)], axis=0)
    pre_own = jnp.concatenate([pres[0], late_own], axis=0)
    pre_sib = jnp.concatenate([pres[1], late_sib], axis=0)
    hid_own = jnp.concatenate([near_hid_own, far_hid_own, late_hid_own], axis=0)
    hid_sib = jnp.concatenate([near_hid_sib, far_hid_sib, late_hid_sib], axis=0)
    scaled = jnp.concatenate([scaled, late_scaled], axis=0)
    rows_home = home[:, :, :width].reshape(slot_count, width)
    active = (keep_mask == 1) & (expert_ids < chips)
    slot_code = jnp.where(active, expert_ids * CAP + slot_ids, -1)
    slot_axis = jnp.arange(slot_count, dtype=jnp.int32)
    pick = (slot_axis == slot_code[:, 0:1]) | (slot_axis == slot_code[:, 1:2])
    in_grad = dot(pick.astype(BF), rows_home, ((1,), (0,))).astype(BF)
    router_grad = jnp.sum(home[:, :, width:].astype(F32), axis=0).T

    in_sib = swap_cores(dot(x_rows, pre_sib, ((0,), (0,))).astype(BF))
    out_sib = swap_cores(dot(hid_sib, scaled, ((0,), (0,))).astype(BF))
    w_in_grad = (dot(x_rows, pre_own, ((0,), (0,))) + in_sib.astype(F32)).astype(BF)[None]
    w_out_grad = (dot(hid_own, scaled, ((0,), (0,))) + out_sib.astype(F32)).astype(BF)[None]
    return (in_grad, w_in_grad, w_out_grad, router_grad)


def solution(mesh):
    experts, groups = mesh.devices.shape
    cut = Mesh(
        mesh.devices.reshape(experts // SPLIT, SPLIT, groups), ("chip", "core", "group")
    )
    by_token = P(("chip", "core", "group"), None)
    by_router = P("group", ("chip", "core"))
    by_in = P(("chip", "core"), None, "group")
    by_out = P(("chip", "core"), "group", None)
    return jax.shard_map(
        body,
        mesh=cut,
        in_specs=(by_token, by_token, by_router, by_in, by_out, by_token, by_token, by_token),
        out_specs=(by_token, by_in, by_out, by_router),
        check_vma=False,
    )
```

```python
import functools

import jax
import jax.numpy as jnp
from jax import lax
from jax.experimental import pallas as pl
from jax.experimental.pallas import tpu as pltpu
from jax.sharding import Mesh
from jax.sharding import PartitionSpec as P

CAP = 2
SPLIT = 2
META = 128
TILE = 256
SWAP = [(0, 1), (1, 0)]
BF = jnp.bfloat16
F32 = jnp.float32
VMEM = pl.BlockSpec(memory_space=pltpu.VMEM)
SMEM = pl.BlockSpec(memory_space=pltpu.SMEM)


def gelu_parts(pre_act):
    cubic_term = 0.044715 * pre_act * pre_act * pre_act
    tanh_value = jnp.tanh(0.7978845608028654 * (pre_act + cubic_term))
    gelu_value = 0.5 * pre_act * (1.0 + tanh_value)
    gelu_slope = 0.5 * (1.0 + tanh_value) + 0.5 * pre_act * (
        1.0 - tanh_value * tanh_value
    ) * 0.7978845608028654 * (1.0 + 3.0 * 0.044715 * pre_act * pre_act)
    return (gelu_value, gelu_slope)


def dot(a, b, dims):
    return lax.dot_general(a, b, (dims, ((), ())), preferred_element_type=F32)


def params():
    return pltpu.CompilerParams(vmem_limit_bytes=24 * 1024 * 1024)


def cost(flops, moved, special=0):
    return pl.CostEstimate(flops=flops, bytes_accessed=moved, transcendentals=special)


def struct(shape, dtype):
    return jax.ShapeDtypeStruct(shape, dtype)


def build_kernel(*refs):
    sources, out_ref, held, sem = refs[:6], refs[6], refs[7:13], refs[13]
    copies = start_copies(zip(sources, held), sem)
    for copy in copies[2:]:
        copy.wait()
    tok_ref, grad_ref, ids_ref, slot_ref, keep_ref, router_ref = held
    slots, width = tok_ref.shape
    part = router_ref.shape[1]
    ids = ids_ref[...]
    active = (keep_ref[...] == 1) & (ids < slots // CAP)
    code = jnp.where(active, ids * CAP + slot_ref[...], -1)
    slot_axis = lax.broadcasted_iota(jnp.int32, (slots, slots), 0)
    first = (slot_axis == code[0:1]).astype(F32)
    second = (slot_axis == code[1:2]).astype(F32)
    place = (first + second).astype(BF)
    wide_ids = ids.astype(F32)
    other = jnp.sum(first * wide_ids[1:2] + second * wide_ids[0:1], axis=1, keepdims=True)
    other = jnp.broadcast_to(other, (slots, META)).astype(BF)
    out_ref[:, 2 * width : 2 * width + META] = other
    even = lax.broadcasted_iota(jnp.int32, (slots, part), 0) % CAP == 0
    router = router_ref[...].astype(F32)
    out_ref[:, 2 * width + META :] = jnp.where(even, router[0:1], router[1:2]).astype(BF)
    copies[0].wait()
    out_ref[:, :width] = dot(place, tok_ref[...], ((1,), (0,))).astype(BF)
    copies[1].wait()
    out_ref[:, width : 2 * width] = dot(place, grad_ref[...], ((1,), (0,))).astype(BF)


def router_kernel(place_ref, r0, r1, r2, r3, router_ref):
    pieces = (r0, r1, r2, r3)
    part = r0.shape[1]
    for i, ref in enumerate(pieces):
        lane = pl.multiple_of((place_ref[0] + i) % len(pieces) * part, part)
        router_ref[:, pl.ds(lane, part)] = ref[...]


def start_copies(pairs, sem):
    copies = [pltpu.make_async_copy(src, dst, sem.at[i]) for i, (src, dst) in enumerate(pairs)]
    for copy in copies:
        copy.start()
    return copies


def parts_of(sets):
    return 2 if sets == 2 else 2 * sets - 2


def tiles_of(refs):
    tiles = []
    for part in range(len(refs)):
        size = refs[part].shape[1]
        shard, first = (part, 0) if part < 2 else (2 + (part - 2) // 2, part % 2 * size)
        tiles += [(shard, first + at, part, at) for at in range(0, size, TILE)]
    return tiles


def expert_kernel(count, sets, *refs):
    parts = parts_of(sets)
    blocks, refs = refs[:count], refs[count:]
    w_ins, w_outs = refs[:parts], refs[parts : 2 * parts]
    hid_own, hid_sib, total_ref = refs[2 * parts : 2 * parts + 3]
    slopes = refs[2 * parts + 3 :]
    width = w_ins[0].shape[0]
    x_rows = jnp.concatenate([ref[:, :width] for ref in blocks], axis=0)
    dy_rows = jnp.concatenate([ref[:, width : 2 * width] for ref in blocks], axis=0)
    hids = (hid_own, hid_sib) + (None,) * (sets - 2)
    total = jnp.zeros((x_rows.shape[0], 1), F32)
    for shard, lane, part, at in tiles_of(w_ins):
        there, here = slice(at, at + TILE), slice(lane, lane + TILE)
        value, slope = gelu_parts(dot(x_rows, w_ins[part][:, there], ((1,), (0,))))
        back_up = dot(dy_rows, w_outs[part][there, :], ((1,), (1,)))
        if hids[shard] is not None:
            hids[shard][:, here] = value.astype(BF)
        slopes[shard][:, here] = back_up * slope
        total += jnp.sum(back_up * value, axis=1, keepdims=True)
    total_ref[...] = jnp.broadcast_to(total, total_ref.shape)


def gates_of(place_ref, own_ref, sib_ref, blocks):
    half, width = own_ref.shape
    core, own_column = place_ref[1], place_ref[2]
    other = jnp.concatenate([ref[:, 2 * width :] for ref in blocks], axis=0)[:, 0:1]
    other = other.astype(F32).astype(jnp.int32)
    pair = other // (CAP * SPLIT) * CAP + other % CAP
    other_column = jnp.where((other // CAP) % SPLIT == core, pair, pair + half)
    axis = lax.broadcasted_iota(jnp.int32, (other.shape[0], 2 * half), 1)
    sign = (axis == own_column).astype(F32) - (axis == other_column).astype(F32)
    x_rows = jnp.concatenate([ref[:, :width] for ref in blocks], axis=0)
    gap = jnp.sum(
        dot(x_rows, own_ref[...], ((1,), (1,))) * sign[:, :half]
        + dot(x_rows, sib_ref[...], ((1,), (1,))) * sign[:, half:],
        axis=1,
        keepdims=True,
    )
    combine = jax.nn.sigmoid(gap)
    return x_rows, sign, combine, combine * jax.nn.sigmoid(-gap)


def scale_rows(gate, blocks, scaled_ref):
    slots, width = blocks[0].shape[0], scaled_ref.shape[1]
    for i, ref in enumerate(blocks):
        here = slice(i * slots, (i + 1) * slots)
        dy_rows = ref[:, width : 2 * width].astype(F32)
        scaled_ref[here, :] = (gate[here] * dy_rows).astype(BF)


def gate_kernel(sets, place_ref, own_ref, sib_ref, b0, b1, near_total, far_total, *refs):
    nears, fars, pres = refs[:sets], refs[sets : 2 * sets], refs[2 * sets : 3 * sets]
    scaled_ref, logit_ref, router_ref = refs[3 * sets :]
    blocks = (b0, b1)
    x_rows, sign, combine, cross = gates_of(place_ref, own_ref, sib_ref, blocks)
    gate = combine.astype(BF).astype(F32)
    slots = b0.shape[0]
    for near_ref, far_ref, pre_ref in zip(nears, fars, pres):
        pre_ref[:slots, :] = (gate[:slots] * near_ref[...]).astype(BF)
        pre_ref[slots:, :] = (gate[slots:] * far_ref[...]).astype(BF)
    total = jnp.concatenate([near_total[:, 0:1], far_total[:, 0:1]], axis=0)
    logit_grad = cross * total * sign
    logit_ref[...] = logit_grad.astype(BF)
    router_ref[...] = dot(logit_grad.T.astype(BF), x_rows, ((1,), (0,))).astype(BF)
    scale_rows(gate, blocks, scaled_ref)


def late_kernel(place_ref, own_ref, sib_ref, b0, b1, own, sib, pre_own, pre_sib, scaled_ref):
    blocks = (b0, b1)
    _, _, combine, _ = gates_of(place_ref, own_ref, sib_ref, blocks)
    gate = combine.astype(BF).astype(F32)
    pre_own[...] = (gate * own[...]).astype(BF)
    pre_sib[...] = (gate * sib[...]).astype(BF)
    scale_rows(gate, blocks, scaled_ref)


def rows_kernel(sets, *refs):
    parts = parts_of(sets)
    pres, w_ins = refs[:sets], refs[sets : sets + parts]
    logit_ref, router_own, router_sib, row_ref = refs[sets + parts :]
    half = router_own.shape[0]
    width = row_ref.shape[1]
    for at in range(0, width, 2 * TILE):
        lanes = slice(at, at + 2 * TILE)
        rows = dot(logit_ref[:, :half], router_own[:, lanes], ((1,), (0,)))
        rows += dot(logit_ref[:, half:], router_sib[:, lanes], ((1,), (0,)))
        for shard, lane, part, first in tiles_of(w_ins):
            weight = w_ins[part][lanes, first : first + TILE]
            rows += dot(pres[shard][:, lane : lane + TILE], weight, ((1,), (1,)))
        row_ref[:, lanes] = rows.astype(BF)


def pack_kernel(place_ref, row_ref, part_ref, recv_ref, keep_ref, far_ref, up_ref, down_ref):
    slots, part = up_ref.shape
    width = row_ref.shape[1]
    groups = width // part
    keep_ref[:, :width] = row_ref[:slots, :]
    far_ref[:, :width] = row_ref[slots:, :]
    for step, ref, at in ((0, keep_ref, width), (2, far_ref, width), (1, up_ref, 0), (3, down_ref, 0)):
        lanes = pl.ds(pl.multiple_of((place_ref[0] + step) % groups * part, part), part)
        ref[:, at : at + part] = (
            part_ref[:slots, lanes].astype(F32) + recv_ref[:, lanes].astype(F32)
        ).astype(BF)


def add_kernel(keep_ref, far_ref, up_ref, down_ref, out_ref):
    width = keep_ref.shape[1] - up_ref.shape[1]
    total = keep_ref[...].astype(F32) + far_ref[...].astype(F32)
    out_ref[:, :width] = total[:, :width].astype(BF)
    side = up_ref[...].astype(F32) + down_ref[...].astype(F32)
    out_ref[:, width:] = (total[:, width:] + side).astype(BF)


def shift_group(value, step):
    count = lax.axis_size("group")
    return lax.ppermute(value, "group", [(i, (i + step) % count) for i in range(count)])


def swap_cores(value):
    return lax.ppermute(value, "core", SWAP)


def call(kernel, out_shape, in_specs, cost_estimate):
    return pl.pallas_call(
        kernel,
        out_shape=out_shape,
        in_specs=in_specs,
        out_specs=jax.tree.map(lambda _: VMEM, out_shape),
        compiler_params=params(),
        cost_estimate=cost_estimate,
    )


def body(tokens, out_grad, w_router, w_in, w_out, expert_ids, slot_ids, keep_mask):
    chips = lax.axis_size("chip")
    groups = lax.axis_size("group")
    chip = lax.axis_index("chip")
    core = lax.axis_index("core")
    group = lax.axis_index("group")
    width = tokens.shape[1]
    hidden = w_in.shape[2]
    slot_count = chips * CAP
    part = w_router.shape[0]
    pair = chip // (CAP * SPLIT) * CAP + chip % CAP
    own_column = jnp.where((chip // CAP) % SPLIT == core, pair, pair + slot_count)
    place = jnp.stack([group, core, own_column]).astype(jnp.int32)

    row_wide = 2 * width + META
    operands = (tokens, out_grad, expert_ids.T, slot_ids.T, keep_mask.T, w_router.T)
    send = pl.pallas_call(
        build_kernel,
        out_shape=struct((slot_count, row_wide + part), BF),
        in_specs=[pl.BlockSpec(memory_space=pl.ANY)] * len(operands),
        out_specs=VMEM,
        scratch_shapes=[pltpu.VMEM(o.shape, o.dtype) for o in operands]
        + [pltpu.SemaphoreType.DMA((len(operands),))],
        compiler_params=pltpu.CompilerParams(vmem_limit_bytes=56 * 1024 * 1024),
        cost_estimate=cost(4 * slot_count * slot_count * width, 4 * slot_count * width * 2),
    )(*operands)

    send, own_in, own_out = lax.optimization_barrier((send, w_in[0], w_out[0]))
    half = hidden // 2
    in_parts, out_parts = [own_in, swap_cores(own_in)], [own_out, swap_cores(own_out)]
    beside_in, beside_out = [], []
    for step in (1, -1):
        at = (group + step) % groups // (groups // 2) * half
        beside_in.append(shift_group(lax.dynamic_slice_in_dim(own_in, at, half, axis=1), step))
        beside_out.append(shift_group(lax.dynamic_slice_in_dim(own_out, at, half, axis=0), step))
    in_parts += beside_in + [swap_cores(w) for w in beside_in]
    out_parts += beside_out + [swap_cores(w) for w in beside_out]
    recv = lax.all_to_all(
        send.reshape(chips, CAP, row_wide + part), "chip", split_axis=0, concat_axis=0, tiled=True
    )
    recv, in_parts, out_parts = lax.optimization_barrier((recv, in_parts, out_parts))
    recv = recv.reshape(slot_count, row_wide + part)
    own_rows = recv[:, :row_wide]
    far_rows = shift_group(own_rows, 2)
    piece = recv[:, row_wide:]
    pieces = [piece, shift_group(piece, -1), shift_group(piece, 2), shift_group(piece, 1)]

    def expert(blocks, sets):
        rows, parts = len(blocks) * slot_count, parts_of(sets)
        return pl.pallas_call(
            functools.partial(expert_kernel, len(blocks), sets),
            out_shape=(struct((rows, hidden), BF),) * 2
            + (struct((rows, META), F32),)
            + (struct((rows, hidden), F32),) * sets,
            in_specs=[VMEM] * (len(blocks) + 2 * parts),
            out_specs=(VMEM,) * (3 + sets),
            compiler_params=params(),
            cost_estimate=cost(4 * rows * width * hidden * sets, rows * width * 8 * sets),
        )(*blocks, *in_parts[:parts], *out_parts[:parts])

    near_hid_own, near_hid_sib, near_total, *nears = expert([own_rows], 4)
    pieces, _ = lax.optimization_barrier((pieces, near_total))
    far_rows, near_total = lax.optimization_barrier((far_rows, near_total))
    router_own = call(
        router_kernel,
        struct((slot_count, width), BF),
        [SMEM] + [VMEM] * 4,
        cost(0, slot_count * width * 4),
    )(place, *pieces)
    router_sib = swap_cores(router_own)
    far_hid_own, far_hid_sib, far_total, *fars = expert([far_rows], 4)
    work_rows = 2 * slot_count
    *pres, scaled, logit_grad, router_part = call(
        functools.partial(gate_kernel, 4),
        (struct((work_rows, hidden), BF),) * 4
        + (
            struct((work_rows, width), BF),
            struct((work_rows, 2 * slot_count), BF),
            struct((2 * slot_count, width), BF),
        ),
        [SMEM] + [VMEM] * 14,
        cost(8 * work_rows * width * slot_count, work_rows * width * 20),
    )(place, router_own, router_sib, own_rows, far_rows, near_total, far_total, *nears, *fars)
    router_recv = swap_cores(router_part[slot_count:])

    row_part = pl.pallas_call(
        functools.partial(rows_kernel, 4),
        out_shape=struct((work_rows, width), BF),
        in_specs=[VMEM] * (4 + parts_of(4) + 3),
        out_specs=VMEM,
        compiler_params=params(),
        cost_estimate=cost(8 * work_rows * width * hidden, work_rows * width * 16),
    )(*pres, *in_parts, logit_grad, router_own, router_sib)
    keep, far_part, up_part, down_part = call(
        pack_kernel,
        (struct((slot_count, width + part), BF),) * 2 + (struct((slot_count, part), BF),) * 2,
        [SMEM] + [VMEM] * 3,
        cost(0, work_rows * width * 4),
    )(place, row_part, router_part, router_recv)
    far_part = shift_group(far_part, 2)
    up_part = shift_group(up_part, 1)
    down_part = shift_group(down_part, -1)
    total = call(
        add_kernel, struct((slot_count, width + part), BF), [VMEM] * 4, cost(0, work_rows * width * 4)
    )(keep, far_part, up_part, down_part)
    total, late_source = lax.optimization_barrier((total.reshape(chips, CAP, width + part), own_rows))
    home = lax.all_to_all(total, "chip", split_axis=0, concat_axis=0, tiled=True)
    late_rows = [shift_group(late_source, -1), shift_group(late_source, 1)]
    late_hid_own, late_hid_sib, _, *lates = expert(late_rows, 2)
    late_own, late_sib, late_scaled = call(
        late_kernel,
        (struct((work_rows, hidden), BF),) * 2 + (struct((work_rows, width), BF),),
        [SMEM] + [VMEM] * 6,
        cost(4 * work_rows * width * slot_count, work_rows * width * 12),
    )(place, router_own, router_sib, *late_rows, *lates)
    rows_dot = lambda a, b: dot(a, b, ((0,), (0,)))
    early_x = jnp.concatenate([own_rows[:, :width], far_rows[:, :width]], axis=0)
    early_hid_own = jnp.concatenate([near_hid_own, far_hid_own], axis=0)
    early_hid_sib = jnp.concatenate([near_hid_sib, far_hid_sib], axis=0)
    _, early_x, pre_own, early_hid_own, early_scaled = lax.optimization_barrier(
        (late_source, early_x, pres[0], early_hid_own, scaled)
    )
    early_in = rows_dot(early_x, pre_own)
    early_out = rows_dot(early_hid_own, early_scaled)
    late_x = jnp.concatenate([r[:, :width] for r in late_rows], axis=0)
    x_rows = jnp.concatenate([early_x, late_x], axis=0)
    scaled = jnp.concatenate([early_scaled, late_scaled], axis=0)
    pre_sib = jnp.concatenate([pres[1], late_sib], axis=0)
    hid_sib = jnp.concatenate([early_hid_sib, late_hid_sib], axis=0)
    in_sib = swap_cores(rows_dot(x_rows, pre_sib).astype(BF)).astype(F32)
    out_sib = swap_cores(rows_dot(hid_sib, scaled).astype(BF)).astype(F32)
    w_in_grad = (early_in + rows_dot(late_x, late_own) + in_sib).astype(BF)[None]
    w_out_grad = (early_out + rows_dot(late_hid_own, late_scaled) + out_sib).astype(BF)[None]
    home, w_in_grad, w_out_grad = lax.optimization_barrier((home, w_in_grad, w_out_grad))
    rows_home = home[:, :, :width].reshape(slot_count, width)
    active = (keep_mask == 1) & (expert_ids < chips)
    slot_code = jnp.where(active, expert_ids * CAP + slot_ids, -1)
    slot_axis = jnp.arange(slot_count, dtype=jnp.int32)
    pick = (slot_axis == slot_code[:, 0:1]) | (slot_axis == slot_code[:, 1:2])
    in_grad = dot(pick.astype(BF), rows_home, ((1,), (0,))).astype(BF)
    router_grad = jnp.sum(home[:, :, width:].astype(F32), axis=0).T

    return (in_grad, w_in_grad, w_out_grad, router_grad)


def solution(mesh):
    experts, groups = mesh.devices.shape
    cut = Mesh(
        mesh.devices.reshape(experts // SPLIT, SPLIT, groups), ("chip", "core", "group")
    )
    by_token = P(("chip", "core", "group"), None)
    by_router = P("group", ("chip", "core"))
    by_in = P(("chip", "core"), None, "group")
    by_out = P(("chip", "core"), "group", None)
    return jax.shard_map(
        body,
        mesh=cut,
        in_specs=(by_token, by_token, by_router, by_in, by_out, by_token, by_token, by_token),
        out_specs=(by_token, by_in, by_out, by_router),
        check_vma=False,
    )
```

```python
import jax
import jax.numpy as jnp
from jax import lax
from jax.experimental import pallas as pl
from jax.experimental.layout import Layout, with_layout_constraint
from jax.experimental.pallas import tpu as pltpu
from jax.sharding import Mesh
from jax.sharding import PartitionSpec as P

CAP = 2
SPLIT = 2
SWAP = [(0, 1), (1, 0)]
BF = jnp.bfloat16
F32 = jnp.float32


def gelu_parts(pre_act):
    cubic_term = 0.044715 * pre_act * pre_act * pre_act
    tanh_value = jnp.tanh(0.7978845608028654 * (pre_act + cubic_term))
    gelu_value = 0.5 * pre_act * (1.0 + tanh_value)
    gelu_slope = 0.5 * (1.0 + tanh_value) + 0.5 * pre_act * (
        1.0 - tanh_value * tanh_value
    ) * 0.7978845608028654 * (1.0 + 3.0 * 0.044715 * pre_act * pre_act)
    return (gelu_value, gelu_slope)


def dot(a, b, dims):
    return lax.dot_general(a, b, (dims, ((), ())), preferred_element_type=F32)


def build_kernel(*refs):
    sources, out_ref, held, sem = refs[:6], refs[6], refs[7:13], refs[13]
    copies = [pltpu.make_async_copy(s, h, sem.at[i]) for i, (s, h) in enumerate(zip(sources, held))]
    for copy in copies:
        copy.start()
    for copy in copies:
        copy.wait()
    tok_ref, grad_ref, ids_ref, slot_ref, keep_ref, router_ref = held
    chips, _, wide = out_ref.shape
    count, width = tok_ref.shape
    part = router_ref.shape[1]
    meta = wide - 2 * width - part
    ids = ids_ref[...]
    active = (keep_ref[...] == 1) & (ids < chips)
    wide_ids = ids.astype(F32)
    chip_axis = lax.broadcasted_iota(jnp.int32, (chips, count), 0)
    slots = []
    for j in range(CAP):
        code = jnp.where(active & (slot_ref[...] == j), ids, -1)
        first = (chip_axis == code[0:1]).astype(F32)
        second = (chip_axis == code[1:2]).astype(F32)
        place = (first + second).astype(BF)
        other = jnp.sum(first * wide_ids[1:2] + second * wide_ids[0:1], axis=1, keepdims=True)
        router = jnp.broadcast_to(router_ref[j : j + 1, :].astype(F32), (chips, part))
        slots.append(
            (
                dot(place, tok_ref[...], ((1,), (0,))),
                dot(place, grad_ref[...], ((1,), (0,))),
                router,
                jnp.broadcast_to(other, (chips, meta)),
            )
        )
    for j, columns in enumerate(slots):
        at = 0
        for column in columns:
            out_ref[:, j, at : at + column.shape[1]] = column.astype(BF)
            at += column.shape[1]


def shift_group(value, step):
    count = lax.axis_size("group")
    return lax.ppermute(value, "group", [(i, (i + step) % count) for i in range(count)])


def swap_cores(value):
    return lax.ppermute(value, "core", SWAP)


def body(tokens, out_grad, w_router, w_in, w_out, expert_ids, slot_ids, keep_mask):
    chips = lax.axis_size("chip")
    groups = lax.axis_size("group")
    chip = lax.axis_index("chip")
    core = lax.axis_index("core")
    group = lax.axis_index("group")
    width = tokens.shape[1]
    slot_count = chips * CAP
    part = w_router.shape[0]

    active = (keep_mask == 1) & (expert_ids < chips)
    slot_code = jnp.where(active, expert_ids * CAP + slot_ids, -1)
    operands = (tokens, out_grad, expert_ids.T, slot_ids.T, keep_mask.T, w_router.T)
    send = pl.pallas_call(
        build_kernel,
        out_shape=jax.ShapeDtypeStruct((chips, CAP, 2 * width + part + 128), BF),
        in_specs=[pl.BlockSpec(memory_space=pl.ANY)] * len(operands),
        out_specs=pl.BlockSpec(memory_space=pltpu.VMEM),
        scratch_shapes=[pltpu.VMEM(o.shape, o.dtype) for o in operands]
        + [pltpu.SemaphoreType.DMA((len(operands),))],
        compiler_params=pltpu.CompilerParams(vmem_limit_bytes=56 * 1024 * 1024),
        cost_estimate=pl.CostEstimate(
            flops=4 * slot_count * slot_count * width,
            bytes_accessed=8 * slot_count * width,
            transcendentals=0,
        ),
    )(*operands)
    send, w_in_own, w_out_own = lax.optimization_barrier((send, w_in[0], w_out[0]))
    w_in_sib, w_out_sib = swap_cores(w_in_own), swap_cores(w_out_own)
    recv = lax.all_to_all(send, "chip", split_axis=0, concat_axis=0, tiled=True)
    recv = with_layout_constraint(
        recv.reshape(slot_count, send.shape[2]), Layout(major_to_minor=(0, 1))
    )

    blocks = [recv, shift_group(recv, -1), shift_group(recv, 2), shift_group(recv, 1)]
    rows = jnp.concatenate(blocks, axis=0)
    x_rows, dy_rows = rows[:, :width], rows[:, width : 2 * width]
    other_id = rows[:, 2 * width + part : 2 * width + part + 1].astype(jnp.int32)

    turned = jnp.concatenate([b[:, 2 * width : 2 * width + part] for b in blocks] * 2, axis=1)
    router_own = lax.dynamic_slice_in_dim(turned, (groups - group) % groups * part, width, axis=1)
    router = jnp.concatenate([router_own, swap_cores(router_own)], axis=0)
    columns = router.shape[0]

    def column_of(expert):
        mine = (expert // CAP) % SPLIT == core
        return jnp.where(mine, 0, columns // 2) + expert // (CAP * SPLIT) * CAP + expert % CAP

    column_axis = jnp.arange(columns, dtype=jnp.int32)[None, :]
    sign = (column_axis == column_of(chip)).astype(F32) - (
        column_axis == column_of(other_id)
    ).astype(F32)
    logits = dot(x_rows, router, ((1,), (1,)))
    gap = jnp.sum(logits * sign, axis=1, keepdims=True)
    combine = jax.nn.sigmoid(gap)
    cross = combine * jax.nn.sigmoid(-gap)
    gate = combine.astype(BF).astype(F32)
    scaled = (gate * dy_rows.astype(F32)).astype(BF)

    gate_grad = 0.0
    row_part = 0.0
    halves = []
    for w_a, w_b in ((w_in_own, w_out_own), (w_in_sib, w_out_sib)):
        gelu_value, gelu_slope = gelu_parts(dot(x_rows, w_a, ((1,), (0,))))
        back_up = dot(dy_rows, w_b, ((1,), (1,)))
        gate_grad = gate_grad + jnp.sum(back_up * gelu_value, axis=1, keepdims=True)
        pre_grad = (gate * back_up * gelu_slope).astype(BF)
        row_part = row_part + dot(pre_grad, w_a, ((1,), (1,)))
        halves.append((pre_grad, gelu_value.astype(BF)))
    logit_grad = (cross * gate_grad * sign).astype(BF)
    row_part = row_part + dot(logit_grad, router, ((1,), (0,)))

    router_part = dot(logit_grad, x_rows, ((0,), (0,)))
    half = columns // 2
    router_part = router_part[:half] + swap_cores(router_part[half:].astype(BF)).astype(F32)
    router_part = router_part.astype(BF)
    router_turned = lax.dynamic_slice_in_dim(
        jnp.concatenate([router_part, router_part], axis=1), group * part, width, axis=1
    )
    row_part = row_part.astype(BF)
    back = [
        jnp.concatenate(
            [
                row_part[i * slot_count : (i + 1) * slot_count],
                router_turned[:, i * part : (i + 1) * part],
            ],
            axis=1,
        )
        for i in range(groups)
    ]
    total = (
        back[0].astype(F32)
        + shift_group(back[1], 1).astype(F32)
        + shift_group(back[2], 2).astype(F32)
        + shift_group(back[3], -1).astype(F32)
    ).astype(BF)
    home = lax.all_to_all(
        total.reshape(chips, CAP, width + part), "chip", split_axis=0, concat_axis=0, tiled=True
    )
    rows_home = home[:, :, :width].reshape(slot_count, width)
    slot_axis = jnp.arange(slot_count, dtype=jnp.int32)
    pick = (slot_axis == slot_code[:, 0:1]) | (slot_axis == slot_code[:, 1:2])
    in_grad = dot(pick.astype(BF), rows_home, ((1,), (0,))).astype(BF)
    router_grad = jnp.sum(home[:, :, width:].astype(F32), axis=0).T

    (pre_own, hid_own), (pre_sib, hid_sib) = halves
    in_sib = swap_cores(dot(x_rows, pre_sib, ((0,), (0,))).astype(BF))
    out_sib = swap_cores(dot(hid_sib, scaled, ((0,), (0,))).astype(BF))
    w_in_grad = (dot(x_rows, pre_own, ((0,), (0,))) + in_sib.astype(F32)).astype(BF)[None]
    w_out_grad = (dot(hid_own, scaled, ((0,), (0,))) + out_sib.astype(F32)).astype(BF)[None]
    return (in_grad, w_in_grad, w_out_grad, router_grad)


def solution(mesh):
    experts, groups = mesh.devices.shape
    cut = Mesh(
        mesh.devices.reshape(experts // SPLIT, SPLIT, groups), ("chip", "core", "group")
    )
    by_token = P(("chip", "core", "group"), None)
    by_router = P("group", ("chip", "core"))
    by_in = P(("chip", "core"), None, "group")
    by_out = P(("chip", "core"), "group", None)
    return jax.shard_map(
        body,
        mesh=cut,
        in_specs=(by_token, by_token, by_router, by_in, by_out, by_token, by_token, by_token),
        out_specs=(by_token, by_in, by_out, by_router),
        check_vma=False,
    )
```

```python
import jax
import jax.numpy as jnp
from jax import lax
from jax.experimental import pallas as pl
from jax.experimental.layout import Layout, with_layout_constraint
from jax.experimental.pallas import tpu as pltpu
from jax.sharding import Mesh
from jax.sharding import PartitionSpec as P

CAP = 2
SPLIT = 2
SWAP = [(0, 1), (1, 0)]
BF = jnp.bfloat16
F32 = jnp.float32


def gelu_parts(pre_act):
    cubic_term = 0.044715 * pre_act * pre_act * pre_act
    tanh_value = jnp.tanh(0.7978845608028654 * (pre_act + cubic_term))
    gelu_value = 0.5 * pre_act * (1.0 + tanh_value)
    gelu_slope = 0.5 * (1.0 + tanh_value) + 0.5 * pre_act * (
        1.0 - tanh_value * tanh_value
    ) * 0.7978845608028654 * (1.0 + 3.0 * 0.044715 * pre_act * pre_act)
    return (gelu_value, gelu_slope)


def dot(a, b, dims):
    return lax.dot_general(a, b, (dims, ((), ())), preferred_element_type=F32)


def build_kernel(*refs):
    sources, out_ref, held, sem = refs[:6], refs[6], refs[7:13], refs[13]
    copies = [pltpu.make_async_copy(s, h, sem.at[i]) for i, (s, h) in enumerate(zip(sources, held))]
    for copy in copies:
        copy.start()
    for copy in copies:
        copy.wait()
    tok_ref, grad_ref, ids_ref, slot_ref, keep_ref, router_ref = held
    chips, _, wide = out_ref.shape
    count, width = tok_ref.shape
    part = router_ref.shape[1]
    meta = wide - 2 * width - part
    ids = ids_ref[...]
    active = (keep_ref[...] == 1) & (ids < chips)
    wide_ids = ids.astype(F32)
    chip_axis = lax.broadcasted_iota(jnp.int32, (chips, count), 0)
    slots = []
    for j in range(CAP):
        code = jnp.where(active & (slot_ref[...] == j), ids, -1)
        first = (chip_axis == code[0:1]).astype(F32)
        second = (chip_axis == code[1:2]).astype(F32)
        place = (first + second).astype(BF)
        other = jnp.sum(first * wide_ids[1:2] + second * wide_ids[0:1], axis=1, keepdims=True)
        router = jnp.broadcast_to(router_ref[j : j + 1, :].astype(F32), (chips, part))
        slots.append(
            (
                dot(place, tok_ref[...], ((1,), (0,))),
                dot(place, grad_ref[...], ((1,), (0,))),
                router,
                jnp.broadcast_to(other, (chips, meta)),
            )
        )
    for j, columns in enumerate(slots):
        at = 0
        for column in columns:
            out_ref[:, j, at : at + column.shape[1]] = column.astype(BF)
            at += column.shape[1]


def sum_kernel(b0, b1, b2, b3, out_ref):
    total = b0[...].astype(F32) + b1[...].astype(F32) + b2[...].astype(F32) + b3[...].astype(F32)
    out_ref[...] = total.reshape(out_ref.shape).astype(BF)


def shift_group(value, step):
    count = lax.axis_size("group")
    return lax.ppermute(value, "group", [(i, (i + step) % count) for i in range(count)])


def swap_cores(value):
    return lax.ppermute(value, "core", SWAP)


def body(tokens, out_grad, w_router, w_in, w_out, expert_ids, slot_ids, keep_mask):
    chips = lax.axis_size("chip")
    groups = lax.axis_size("group")
    chip = lax.axis_index("chip")
    core = lax.axis_index("core")
    group = lax.axis_index("group")
    width = tokens.shape[1]
    slot_count = chips * CAP
    part = w_router.shape[0]

    active = (keep_mask == 1) & (expert_ids < chips)
    slot_code = jnp.where(active, expert_ids * CAP + slot_ids, -1)
    operands = (tokens, out_grad, expert_ids.T, slot_ids.T, keep_mask.T, w_router.T)
    send = pl.pallas_call(
        build_kernel,
        out_shape=jax.ShapeDtypeStruct((chips, CAP, 2 * width + part + 128), BF),
        in_specs=[pl.BlockSpec(memory_space=pl.ANY)] * len(operands),
        out_specs=pl.BlockSpec(memory_space=pltpu.VMEM),
        scratch_shapes=[pltpu.VMEM(o.shape, o.dtype) for o in operands]
        + [pltpu.SemaphoreType.DMA((len(operands),))],
        compiler_params=pltpu.CompilerParams(vmem_limit_bytes=56 * 1024 * 1024),
        cost_estimate=pl.CostEstimate(
            flops=4 * slot_count * slot_count * width,
            bytes_accessed=8 * slot_count * width,
            transcendentals=0,
        ),
    )(*operands)
    send, w_in_own, w_out_own = lax.optimization_barrier((send, w_in[0], w_out[0]))
    w_in_sib, w_out_sib = swap_cores(w_in_own), swap_cores(w_out_own)
    recv = lax.all_to_all(send, "chip", split_axis=0, concat_axis=0, tiled=True)
    recv = with_layout_constraint(
        recv.reshape(slot_count, send.shape[2]), Layout(major_to_minor=(0, 1))
    )

    blocks = [recv, shift_group(recv, -1), shift_group(recv, 2), shift_group(recv, 1)]
    rows = jnp.concatenate(blocks, axis=0)
    x_rows, dy_rows = rows[:, :width], rows[:, width : 2 * width]
    other_id = rows[:, 2 * width + part : 2 * width + part + 1].astype(jnp.int32)

    turned = jnp.concatenate([b[:, 2 * width : 2 * width + part] for b in blocks] * 2, axis=1)
    router_own = lax.dynamic_slice_in_dim(turned, (groups - group) % groups * part, width, axis=1)
    router = jnp.concatenate([router_own, swap_cores(router_own)], axis=0)
    columns = router.shape[0]

    def column_of(expert):
        mine = (expert // CAP) % SPLIT == core
        return jnp.where(mine, 0, columns // 2) + expert // (CAP * SPLIT) * CAP + expert % CAP

    column_axis = jnp.arange(columns, dtype=jnp.int32)[None, :]
    sign = (column_axis == column_of(chip)).astype(F32) - (
        column_axis == column_of(other_id)
    ).astype(F32)
    logits = dot(x_rows, router, ((1,), (1,)))
    gap = jnp.sum(logits * sign, axis=1, keepdims=True)
    combine = jax.nn.sigmoid(gap)
    cross = combine * jax.nn.sigmoid(-gap)
    gate = combine.astype(BF).astype(F32)
    scaled = (gate * dy_rows.astype(F32)).astype(BF)

    gate_grad = 0.0
    row_part = 0.0
    halves = []
    for w_a, w_b in ((w_in_own, w_out_own), (w_in_sib, w_out_sib)):
        gelu_value, gelu_slope = gelu_parts(dot(x_rows, w_a, ((1,), (0,))))
        back_up = dot(dy_rows, w_b, ((1,), (1,)))
        gate_grad = gate_grad + jnp.sum(back_up * gelu_value, axis=1, keepdims=True)
        pre_grad = (gate * back_up * gelu_slope).astype(BF)
        row_part = row_part + dot(pre_grad, w_a, ((1,), (1,)))
        halves.append((pre_grad, gelu_value.astype(BF)))
    logit_grad = (cross * gate_grad * sign).astype(BF)
    row_part = row_part + dot(logit_grad, router, ((1,), (0,)))

    router_part = dot(logit_grad, x_rows, ((0,), (0,)))
    half = columns // 2
    router_part = router_part[:half] + swap_cores(router_part[half:].astype(BF)).astype(F32)
    router_part = router_part.astype(BF)
    router_turned = lax.dynamic_slice_in_dim(
        jnp.concatenate([router_part, router_part], axis=1), group * part, width, axis=1
    )
    row_part = row_part.astype(BF)
    back = [
        jnp.concatenate(
            [
                row_part[i * slot_count : (i + 1) * slot_count],
                router_turned[:, i * part : (i + 1) * part],
            ],
            axis=1,
        )
        for i in range(groups)
    ]
    parts = (
        back[0],
        shift_group(back[1], 1),
        shift_group(back[2], 2),
        shift_group(back[3], -1),
    )
    vmem = pl.BlockSpec(memory_space=pltpu.VMEM)
    total = pl.pallas_call(
        sum_kernel,
        out_shape=jax.ShapeDtypeStruct((chips, CAP, width + part), BF),
        in_specs=[vmem] * groups,
        out_specs=vmem,
        compiler_params=pltpu.CompilerParams(vmem_limit_bytes=16 * 1024 * 1024),
        cost_estimate=pl.CostEstimate(
            flops=4 * slot_count * width, bytes_accessed=16 * slot_count * width, transcendentals=0
        ),
    )(*parts)
    home = lax.all_to_all(total, "chip", split_axis=0, concat_axis=0, tiled=True)
    rows_home = home[:, :, :width].reshape(slot_count, width)
    slot_axis = jnp.arange(slot_count, dtype=jnp.int32)
    pick = (slot_axis == slot_code[:, 0:1]) | (slot_axis == slot_code[:, 1:2])
    in_grad = dot(pick.astype(BF), rows_home, ((1,), (0,))).astype(BF)
    router_grad = jnp.sum(home[:, :, width:].astype(F32), axis=0).T

    (pre_own, hid_own), (pre_sib, hid_sib) = halves
    in_sib = swap_cores(dot(x_rows, pre_sib, ((0,), (0,))).astype(BF))
    out_sib = swap_cores(dot(hid_sib, scaled, ((0,), (0,))).astype(BF))
    w_in_grad = (dot(x_rows, pre_own, ((0,), (0,))) + in_sib.astype(F32)).astype(BF)[None]
    w_out_grad = (dot(hid_own, scaled, ((0,), (0,))) + out_sib.astype(F32)).astype(BF)[None]
    return (in_grad, w_in_grad, w_out_grad, router_grad)


def solution(mesh):
    experts, groups = mesh.devices.shape
    cut = Mesh(
        mesh.devices.reshape(experts // SPLIT, SPLIT, groups), ("chip", "core", "group")
    )
    by_token = P(("chip", "core", "group"), None)
    by_router = P("group", ("chip", "core"))
    by_in = P(("chip", "core"), None, "group")
    by_out = P(("chip", "core"), "group", None)
    return jax.shard_map(
        body,
        mesh=cut,
        in_specs=(by_token, by_token, by_router, by_in, by_out, by_token, by_token, by_token),
        out_specs=(by_token, by_in, by_out, by_router),
        check_vma=False,
    )
```
